256 devices in a mesh: date: 32 (over y, z_hi, core), tile: 8 (over z_lo, x).
Axes of the slice: x: 4, y: 4, z: 8 (z_hi: 4, z_lo: 2; z = z_hi * 2 + z_lo), core: 2. Of those that a mesh axis runs over, the one named last changes fastest.
Arguments:
- latest_model_output: float32 [2, 24, 16, 64, 128], P(None, None, None, 'tile', 'date'), may hold values from -6 to 6
- bygone_model_outputs: float32 [128, 24, 16, 64, 128], P('date', None, None, 'tile'), may hold values from -6 to 6
- sensor_reports: float32 [128, 24, 64, 128], P('date', None, 'tile'), may hold values from -6 to 6
- input_variable_scaling: float32 [16], replicated, may hold values from 0.25 to 4
- stepahead_blur_scale: float32 [24], replicated, may hold values from 0.02 to 0.08
- bygone_annual_ordinal: int32 [128], P('date'), may hold values from 0 to 364
- launch_annual_ordinal: int32 [2], replicated, may hold values from 0 to 364
Outputs:
- analog_mean: float32 [2, 24, 64, 128], P(None, None, 'tile', 'date')
The draws below stay inside these ranges and needn't reach their ends.
All inputs are finite; a program needn't handle non-finite values.
Results may differ from the reference program's by a relative error of at most 0.0003.
Values sent between devices are 32-bit elements; how exact they have to be, the bound alone decides.
A program may use at most 128 MiB of HBM per device.

```python
import math
import jax
import jax.numpy as jnp
from jax import lax

INPUT_VARIABLES = 16
STEP_AHEAD_COUNT = 24
WIN_HALF = 3
CYCLES = 2
ARCHIVED_SAMPLES = 128
GRID_NORTHWARD = 64
GRID_EASTWARD = 128


def draw_latest_model_output(key, part):
    base_key = jax.random.fold_in(key, 11)
    extent = (CYCLES, STEP_AHEAD_COUNT, INPUT_VARIABLES, GRID_NORTHWARD, GRID_EASTWARD)
    values = jax.random.normal(base_key, extent, jnp.float32)
    return jnp.clip(values, -6.0, 6.0)


def expand_blocks(field):
    field = jnp.repeat(field, 8, axis=1)[:, :STEP_AHEAD_COUNT]
    field = jnp.repeat(field, 4, axis=3)[:, :, :, :GRID_NORTHWARD]
    field = jnp.repeat(field, 8, axis=4)[:, :, :, :, :GRID_EASTWARD]
    return field


def draw_bygone_model_outputs(key, part):
    extent = (ARCHIVED_SAMPLES, STEP_AHEAD_COUNT, INPUT_VARIABLES, GRID_NORTHWARD, GRID_EASTWARD)
    lead_blocks = (STEP_AHEAD_COUNT + 7) // 8
    row_blocks = (GRID_NORTHWARD + 3) // 4
    col_blocks = (GRID_EASTWARD + 7) // 8
    common = jax.random.uniform(jax.random.fold_in(key, 21), (1, lead_blocks, 1, row_blocks, col_blocks), jnp.float32, -3.0, 3.0)
    per_date = jax.random.uniform(jax.random.fold_in(key, 22), (ARCHIVED_SAMPLES, lead_blocks, 1, row_blocks, 1), jnp.float32, -1.0, 1.0)
    common_full = expand_blocks(common)
    per_date_full = expand_blocks(jnp.broadcast_to(per_date, (ARCHIVED_SAMPLES, lead_blocks, 1, row_blocks, col_blocks)))
    noise_key = jax.random.fold_in(key, 23)
    noise = jax.random.normal(noise_key, extent, jnp.float32)
    return jnp.clip(noise + common_full + per_date_full, -6.0, 6.0)


def with_ends(array, own_key, low, largest):
    dims = array.shape
    spot = [jax.random.randint(jax.random.fold_in(own_key, axis), (), 0, dims[axis]) for axis in range(len(dims))]
    array = array.at[tuple(spot)].set(low)
    longest = dims.index(max(dims))
    spot[longest] = (spot[longest] + 1) % dims[longest]
    return array.at[tuple(spot)].set(largest)


def level_of(own_key, shape, cuts, low, top_value):
    gain, own = 1.0, jax.random.fold_in(own_key, 6)
    for position, parts in cuts:
        heights = jnp.exp(jax.random.uniform(jax.random.fold_in(own, position), (parts,), jnp.float32, low / len(cuts), top_value / len(cuts)))
        gain = gain * jnp.repeat(heights, shape[position] // parts).reshape([-1 if axis == position else 1 for axis in range(len(shape))])
    return gain


def normal_values(rng, shape, scale, bound, pieces=(), held_as=jnp.bfloat16):
    drawn = scale * jax.random.normal(rng, shape, jnp.float32)
    if pieces:
        drawn = drawn * level_of(rng, shape, pieces, -0.22, 0.18)
    return jnp.clip(drawn, -bound, bound).astype(held_as)


def setup_inputs(seed: int = 0) -> dict:
    key_list = jax.random.split(jax.random.key(seed), 8)
    latest_model_output = draw_latest_model_output(jax.random.fold_in(key_list[7], 71), 0)
    bygone_model_outputs = draw_bygone_model_outputs(jax.random.fold_in(key_list[7], 71), 0)
    sensor_reports = normal_values(key_list[2], (ARCHIVED_SAMPLES, STEP_AHEAD_COUNT, GRID_NORTHWARD, GRID_EASTWARD), 1.0, 6.0, ((0, 32), (2, 8)), jnp.float32)
    input_variable_scaling = jnp.clip(jnp.exp(jax.random.uniform(key_list[3], (INPUT_VARIABLES,), jnp.float32, math.log(0.25), math.log(4.0))), 0.25, 4.0)
    stepahead_blur_scale = jnp.clip(jnp.exp(jax.random.uniform(key_list[4], (STEP_AHEAD_COUNT,), jnp.float32, math.log(0.02), math.log(0.08))), 0.02, 0.08)
    bygone_annual_ordinal = with_ends(jax.random.randint(key_list[5], (ARCHIVED_SAMPLES,), 0, 365), jax.random.fold_in(key_list[5], 1), 0, 364).astype(jnp.int32)
    launch_annual_ordinal = jax.random.randint(key_list[6], (CYCLES,), 0, 365).astype(jnp.int32)
    return {"latest_model_output": latest_model_output, "bygone_model_outputs": bygone_model_outputs, "sensor_reports": sensor_reports, "input_variable_scaling": input_variable_scaling, "stepahead_blur_scale": stepahead_blur_scale, "bygone_annual_ordinal": bygone_annual_ordinal, "launch_annual_ordinal": launch_annual_ordinal}


season_gain = 0.5


def window_sum(diffsq, reach):
    lead_count = diffsq.shape[-3]
    row_count = diffsq.shape[-2]
    col_count = diffsq.shape[-1]
    padded = jnp.pad(diffsq, [(0, 0)] * (diffsq.ndim - 3) + [(reach, reach), (1, 1), (1, 1)])
    totals = jnp.zeros(diffsq.shape, jnp.float32)
    for offset in range(2 * reach + 1):
        for row_off in range(3):
            for col_off in range(3):
                totals = totals + padded[..., offset:offset + lead_count, row_off:row_off + row_count, col_off:col_off + col_count]
    return totals / (9.0 * (2 * reach + 1))


def reference(latest_model_output, bygone_model_outputs, sensor_reports, input_variable_scaling, stepahead_blur_scale, bygone_annual_ordinal, launch_annual_ordinal):
    def single_sample(element):
        bygone_sample, calendar = element
        feature_discrepancy = latest_model_output - bygone_sample[None]
        diffsq = jnp.sum(feature_discrepancy * feature_discrepancy * input_variable_scaling[None, None, :, None, None], axis=2) / INPUT_VARIABLES
        season = season_gain * (1.0 - jnp.cos(2.0 * math.pi * (calendar - launch_annual_ordinal).astype(jnp.float32) / 365.0))
        return window_sum(diffsq, WIN_HALF) + season[:, None, None, None]

    analog_metric = lax.map(single_sample, (bygone_model_outputs, bygone_annual_ordinal))
    nearest = jnp.min(analog_metric, axis=0)
    spread_lead = stepahead_blur_scale[None, :, None, None]

    def accumulate(totals, element):
        distance, observed_day = element
        kernel = jnp.exp(-(distance - nearest) / spread_lead)
        return (totals[0] + kernel * observed_day[None], totals[1] + kernel), None

    zeros_field = jnp.zeros(nearest.shape, jnp.float32)
    (numer, denom), _ = lax.scan(accumulate, (zeros_field, zeros_field), (analog_metric, sensor_reports))
    return numer / denom
```

```python
import functools
import math

import jax
import jax.numpy as jnp
from jax import lax
from jax.experimental import pallas as pl
from jax.experimental.pallas import tpu as pltpu
from jax.sharding import PartitionSpec as P

MESH = pl.DeviceIdType.MESH
LEADS = 24
REACH = 3
CHUNKS = ((0, 4), (4, 4), (8, 4), (12, 4), (16, 4), (20, 4))
BLOCK = 8
BLOCKS = LEADS // BLOCK


def remote(src, dst, send, recv, device):
    return pltpu.make_async_remote_copy(
        src_ref=src, dst_ref=dst, send_sem=send, recv_sem=recv, device_id=device, device_id_type=MESH
    )


def kernel(
    cur_hbm, arch_hbm, obs_hbm, w_ref, blur_ref, cal_ref, today_ref,
    out_ref,
    cur_in, arch, obs, stage, landed, gath, curr, dw, edge_lo, edge_hi, halo_up, halo_dn, season, parts, other, pack, packed,
    pieces, ends,
    local_sem, arch_sem, pair_sem, z_send, z_recv, y_send, y_recv, c_send, c_recv, h_send, h_recv, p_send, p_recv,
    r_send, r_recv, e_send, e_recv,
):
    date, tile = lax.axis_index("date"), lax.axis_index("tile")
    row, depth, core = date // 8, (date // 2) % 4, date % 2
    chip = row * 4 + depth
    tiles = 8

    def at(dy, dz):
        return ((((row + dy) % 4) * 4 + (depth + dz) % 4) * 2 + core, tile)

    def chip_at(dy, dz):
        return ((row + dy) % 4) * 4 + (depth + dz) % 4

    partner = (date + 1 - 2 * core, tile)
    others = [(dy, dz) for dy in range(4) for dz in range(4) if (dy, dz) != (0, 0)]

    load_cur = pltpu.make_async_copy(cur_hbm, cur_in, local_sem.at[0])
    load_cur.start()
    barrier = pltpu.get_barrier_semaphore()
    for dy, dz in others:
        pl.semaphore_signal(barrier, inc=1, device_id=at(dy, dz), device_id_type=MESH)
    pl.semaphore_signal(barrier, inc=1, device_id=partner, device_id_type=MESH)

    @pl.when(tile > 0)
    def _():
        pl.semaphore_signal(barrier, inc=1, device_id=(date, tile - 1), device_id_type=MESH)

    @pl.when(tile < tiles - 1)
    def _():
        pl.semaphore_signal(barrier, inc=1, device_id=(date, tile + 1), device_id_type=MESH)

    loads = []
    for j, (t0, n) in enumerate(CHUNKS):
        copy = pltpu.make_async_copy(arch_hbm.at[:, pl.ds(t0, n)], arch.at[:, pl.ds(t0, n)], arch_sem.at[j])
        copy.start()
        loads.append(copy)
    load_obs = pltpu.make_async_copy(obs_hbm, obs, local_sem.at[1])
    load_obs.start()

    load_cur.wait()
    for x in range(4):
        for mine in range(2):
            cycle = core if mine else 1 - core
            values = cur_in[cycle, :, :, x, :].reshape(128, LEADS).T
            if mine:
                gath[:, chip, core * 4 + x, :] = values
            else:
                stage[:, x, :] = values

    pl.semaphore_wait(barrier, 16 + jnp.where(tile > 0, 1, 0) + jnp.where(tile < tiles - 1, 1, 0))

    pair = remote(stage, landed, pair_sem.at[0], pair_sem.at[1], partner)
    pair.start()

    zero = jnp.zeros((8, 128), jnp.float32)
    for k in range(REACH):
        for side in (k, LEADS + REACH + k):
            for i in range(8):
                dw[side, i] = zero
            halo_up[side] = zero
            halo_dn[side] = zero

    @pl.when(tile == 0)
    def _():
        for t in range(LEADS):
            halo_up[REACH + t] = zero

    @pl.when(tile == tiles - 1)
    def _():
        for t in range(LEADS):
            halo_dn[REACH + t] = zero

    sub = lax.broadcasted_iota(jnp.int32, (8, 128), 0)
    lane = lax.broadcasted_iota(jnp.int32, (8, 128), 1)
    days = jnp.zeros((8, 128), jnp.float32)
    for i in range(8):
        gap = (cal_ref[i % 4] - today_ref[i // 4]).astype(jnp.float32)
        days = jnp.where(sub == i, gap, days)
    season[...] = 0.5 * (1.0 - jnp.cos(2.0 * math.pi * days / 365.0))

    pair.wait_recv()
    for x in range(4):
        gath[:, chip, (1 - core) * 4 + x, :] = landed[:, x, :]

    def z_copy(j, dz):
        t0, n = CHUNKS[j]
        return remote(
            gath.at[pl.ds(t0, n), chip], gath.at[pl.ds(t0, n), chip],
            z_send.at[j, dz - 1], z_recv.at[j, dz - 1], at(0, dz),
        )

    def z_wait(j, dz):
        t0, n = CHUNKS[j]
        here = gath.at[pl.ds(t0, n), chip_at(0, 4 - dz)]
        remote(here, here, z_send.at[j, dz - 1], z_recv.at[j, dz - 1], at(0, dz)).wait_recv()

    def y_copy(j, dy):
        t0, n = CHUNKS[j]
        plane = gath.at[pl.ds(t0, n), pl.ds(row * 4, 4)]
        return remote(plane, plane, y_send.at[j, dy - 1], y_recv.at[j, dy - 1], at(dy, 0))

    def y_wait(j, dy):
        t0, n = CHUNKS[j]
        plane = gath.at[pl.ds(t0, n), pl.ds(((row + 4 - dy) % 4) * 4, 4)]
        remote(plane, plane, y_send.at[j, dy - 1], y_recv.at[j, dy - 1], at(dy, 0)).wait_recv()

    def c_copy(j, cycle):
        t0, n = CHUNKS[j]
        block = curr.at[cycle, pl.ds(t0, n)]
        return remote(block, block, c_send.at[j], c_recv.at[j], partner)

    def h_copy(j, up):
        t0, n = CHUNKS[j]
        if up:
            return remote(
                edge_hi.at[pl.ds(t0, n)], halo_up.at[pl.ds(REACH + t0, n)], h_send.at[j, 0], h_recv.at[j, 0], (date, tile + 1)
            )
        return remote(
            edge_lo.at[pl.ds(t0, n)], halo_dn.at[pl.ds(REACH + t0, n)], h_send.at[j, 1], h_recv.at[j, 1], (date, tile - 1)
        )

    def p_copy(b):
        return remote(
            parts.at[1 - core, pl.ds(b * BLOCK, BLOCK)], other.at[pl.ds(b * BLOCK, BLOCK)], p_send.at[b], p_recv.at[b], partner
        )

    def r_copy(b, o):
        dy, dz = others[o]
        return remote(packed.at[b, chip_at(dy, dz)], pieces.at[b, o], r_send.at[b], r_recv.at[b], at(dy, dz))

    for j in range(len(CHUNKS)):
        for dz in (2, 1, 3):
            z_copy(j, dz).start()
    for j in range(len(CHUNKS)):
        for dz in (1, 3, 2):
            z_wait(j, dz)
        for dy in (2, 1, 3):
            y_copy(j, dy).start()

    def transpose(j):
        t0, n = CHUNKS[j]
        for dy in (1, 3, 2):
            y_wait(j, dy)

        def turn(t, carry):
            curr[core, t] = gath[t].reshape(128, 128).T.reshape(16, 8, 128)
            return carry

        lax.fori_loop(t0, t0 + n, turn, 0)
        c_copy(j, core).start()

    def differences(j):
        t0, n = CHUNKS[j]
        loads[j].wait()
        c_copy(j, 1 - core).wait_recv()

        def one(t, carry):
            for d in range(4):
                sums = [None, None]
                for p in range(16):
                    past = arch[d, t, p]
                    for c in range(2):
                        gap = curr[c, t, p] - past
                        term = gap * gap * w_ref[p]
                        sums[c] = term if p == 0 else sums[c] + term
                for c in range(2):
                    v = sums[c]
                    v = (
                        v
                        + jnp.where(lane > 0, pltpu.roll(v, 1, 1), 0.0)
                        + jnp.where(lane < 127, pltpu.roll(v, 127, 1), 0.0)
                    )
                    i = c * 4 + d
                    dw[t + REACH, i] = v
                    edge_lo[t, pl.ds(i, 1)] = v[0:1]
                    edge_hi[t, pl.ds(i, 1)] = v[7:8]
            return carry

        lax.fori_loop(t0, t0 + n, one, 0)

        @pl.when(tile < tiles - 1)
        def _():
            h_copy(j, True).start()

        @pl.when(tile > 0)
        def _():
            h_copy(j, False).start()

    done = [0]
    sent = [0]

    def scores(j):
        t0, n = CHUNKS[j]
        last = j == len(CHUNKS) - 1
        stop = LEADS if last else t0 + n - REACH
        if j == 0:
            load_obs.wait()

        @pl.when(tile > 0)
        def _():
            h_copy(j, True).wait_recv()

        @pl.when(tile < tiles - 1)
        def _():
            h_copy(j, False).wait_recv()

        def one(t, carry):
            above, below = halo_up[t], halo_dn[t]
            for k in range(1, 2 * REACH + 1):
                above = above + halo_up[t + k]
                below = below + halo_dn[t + k]
            spread = blur_ref[t]
            for c in range(2):
                dist = []
                for d in range(4):
                    i = c * 4 + d
                    v = dw[t, i]
                    for k in range(1, 2 * REACH + 1):
                        v = v + dw[t + k, i]
                    up = jnp.where(sub == 0, jnp.broadcast_to(above[i : i + 1], (8, 128)), pltpu.roll(v, 1, 0))
                    down = jnp.where(sub == 7, jnp.broadcast_to(below[i : i + 1], (8, 128)), pltpu.roll(v, 7, 0))
                    v = (v + up + down) * (1.0 / (16.0 * 9.0 * (2 * REACH + 1)))
                    dist.append(v + jnp.broadcast_to(season[pl.ds(i, 1)], (8, 128)))
                low = jnp.minimum(jnp.minimum(dist[0], dist[1]), jnp.minimum(dist[2], dist[3]))
                den = num = None
                for d in range(4):
                    e = jnp.exp((low - dist[d]) / spread)
                    f = e * obs[d, t]
                    den = e if d == 0 else den + e
                    num = f if d == 0 else num + f
                parts[c, t, 0] = low - spread * jnp.log(den)
                parts[c, t, 1] = num / den
            return carry

        lax.fori_loop(done[0], stop, one, 0)
        done[0] = stop
        while sent[0] < BLOCKS and done[0] >= (sent[0] + 1) * BLOCK:
            p_copy(sent[0]).start()
            sent[0] += 1

    def combine(b):
        p_copy(b).wait_recv()

        def one(s, carry):
            t = b * BLOCK + s
            spread = blur_ref[t]
            a0, r0 = parts[core, t, 0], parts[core, t, 1]
            a1, r1 = other[t, 0], other[t, 1]
            low = jnp.minimum(a0, a1)
            e0, e1 = jnp.exp((low - a0) / spread), jnp.exp((low - a1) / spread)
            den = e0 + e1
            pack[0, :, s, :] = low - spread * jnp.log(den)
            pack[1, :, s, :] = (e0 * r0 + e1 * r1) / den
            return carry

        lax.fori_loop(0, BLOCK, one, 0)
        packed[b] = pack[...].reshape(128, 128).T.reshape(16, 8, 128)
        for o in range(15):
            r_copy(b, o).start()

    combined = 0
    for j in range(len(CHUNKS)):
        transpose(j)
        if j > 0:
            before = sent[0]
            while combined < before:
                combine(combined)
                combined += 1
            scores(j - 1)
        differences(j)
    scores(len(CHUNKS) - 1)
    while combined < BLOCKS:
        combine(combined)
        combined += 1

    for b in range(BLOCKS):
        here = pieces.at[b]
        remote(here, here, r_send.at[b], r_recv.at[b], partner).wait_recv()
        spread = jnp.zeros((8, 128), jnp.float32)
        for s in range(BLOCK):
            spread = jnp.where(lane % BLOCK == s, blur_ref[b * BLOCK + s], spread)
        terms = [packed[b, chip]] + [pieces[b, o] for o in range(15)]
        low = functools.reduce(jnp.minimum, terms)
        den = num = None
        for i, v in enumerate(terms):
            e = jnp.exp((low - v) / spread)
            f = pltpu.roll(e, 64, 1) * v
            den = e if i == 0 else den + e
            num = f if i == 0 else num + f
        ends[core, b] = num / pltpu.roll(den, 64, 1)

    swap = remote(ends.at[core], ends.at[core], e_send, e_recv, partner)
    swap.start()
    other_ends = remote(ends.at[1 - core], ends.at[1 - core], e_send, e_recv, partner)
    other_ends.wait_recv()
    for c in range(2):
        blocks = []
        for b in range(BLOCKS):
            v = ends[c, b]
            blocks.append(jnp.where(core == 0, v, pltpu.roll(v, 4, 0)))
        for y in range(8):
            v = jnp.zeros((8, 128), jnp.float32)
            for b in range(BLOCKS):
                shift = (b * BLOCK - 64 - y * BLOCK) % 128
                moved = blocks[b] if shift == 0 else pltpu.roll(blocks[b], shift, 1)
                v = jnp.where(lane // BLOCK == b, moved, v)
            out_ref[c, y] = v[0:4, 0:LEADS]

    pair.wait_send()
    swap.wait_send()
    for j in range(len(CHUNKS)):
        for d in (1, 2, 3):
            z_copy(j, d).wait_send()
            y_copy(j, d).wait_send()
        c_copy(j, core).wait_send()

    @pl.when(tile < tiles - 1)
    def _():
        for j in range(len(CHUNKS)):
            h_copy(j, True).wait_send()

    @pl.when(tile > 0)
    def _():
        for j in range(len(CHUNKS)):
            h_copy(j, False).wait_send()

    for b in range(BLOCKS):
        p_copy(b).wait_send()
        here = pieces.at[b]
        remote(here, here, r_send.at[b], r_recv.at[b], partner).wait_send()


def local(current, archive, reports, weights, blur, calendar, today):
    count = len(CHUNKS)
    f32 = jnp.float32
    dma = pltpu.SemaphoreType.DMA
    leads = LEADS + 2 * REACH
    out = pl.pallas_call(
        kernel,
        out_shape=jax.ShapeDtypeStruct((2, 8, 4, LEADS), f32),
        in_specs=[pl.BlockSpec(memory_space=pl.ANY)] * 3 + [pl.BlockSpec(memory_space=pltpu.SMEM)] * 4,
        out_specs=pl.BlockSpec(memory_space=pltpu.VMEM),
        scratch_shapes=[
            pltpu.VMEM((2, 16, 8, 4, LEADS), f32),
            pltpu.VMEM((4, LEADS, 16, 8, 128), f32),
            pltpu.VMEM((4, LEADS, 8, 128), f32),
            pltpu.VMEM((LEADS, 4, 128), f32),
            pltpu.VMEM((LEADS, 4, 128), f32),
            pltpu.VMEM((LEADS, 16, 8, 128), f32),
            pltpu.VMEM((2, LEADS, 16, 8, 128), f32),
            pltpu.VMEM((leads, 8, 8, 128), f32),
            pltpu.VMEM((LEADS, 8, 128), f32),
            pltpu.VMEM((LEADS, 8, 128), f32),
            pltpu.VMEM((leads, 8, 128), f32),
            pltpu.VMEM((leads, 8, 128), f32),
            pltpu.VMEM((8, 128), f32),
            pltpu.VMEM((2, LEADS, 2, 8, 128), f32),
            pltpu.VMEM((LEADS, 2, 8, 128), f32),
            pltpu.VMEM((2, 8, BLOCK, 128), f32),
            pltpu.VMEM((BLOCKS, 16, 8, 128), f32),
            pltpu.VMEM((BLOCKS, 15, 8, 128), f32),
            pltpu.VMEM((2, BLOCKS, 8, 128), f32),
            dma((2,)),
            dma((count,)),
            dma((2,)),
            dma((count, 3)), dma((count, 3)),
            dma((count, 3)), dma((count, 3)),
            dma((count,)), dma((count,)),
            dma((count, 2)), dma((count, 2)),
            dma((BLOCKS,)), dma((BLOCKS,)),
            dma((BLOCKS,)), dma((BLOCKS,)),
            dma, dma,
        ],
        compiler_params=pltpu.CompilerParams(
            collective_id=0, has_side_effects=True, vmem_limit_bytes=40 * 2**20
        ),
    )(jnp.transpose(current, (0, 2, 3, 4, 1)), archive, reports, weights, blur, calendar, today)
    return jnp.transpose(out, (0, 3, 1, 2))


def solution(mesh):
    placed = (
        P(None, None, None, "tile", "date"),
        P("date", None, None, "tile", None),
        P("date", None, "tile", None),
        P(),
        P(),
        P("date"),
        P(),
    )
    return jax.shard_map(
        local, mesh=mesh, in_specs=placed, out_specs=P(None, None, "tile", "date"), check_vma=False
    )
```

```python
import functools
import math

import jax
import jax.numpy as jnp
from jax import lax
from jax.experimental import pallas as pl
from jax.experimental.pallas import tpu as pltpu
from jax.sharding import PartitionSpec as P

MESH = pl.DeviceIdType.MESH
LEADS = 24
REACH = 3
CHUNKS = ((6, 6, False), (12, 6, False), (18, 6, False), (0, 6, True))
STEPS = (
    ("F", 3), ("F", 0), ("F", 1), ("R", 0), ("F", 2), ("R", 1), ("T", 0), ("R", 2), ("T", 1), ("D", 0), ("T", 3), ("D", 1), ("S", 0), ("T", 2), ("D", 3), ("S", 1), ("D", 2), ("S", 3), ("S", 2),
)
BLOCK = 8
BLOCKS = LEADS // BLOCK


def remote(src, dst, send, recv, device):
    return pltpu.make_async_remote_copy(
        src_ref=src, dst_ref=dst, send_sem=send, recv_sem=recv, device_id=device, device_id_type=MESH
    )


def kernel(
    cur_hbm, arch_hbm, obs_hbm, w_hbm, blur_hbm, cal_hbm, today_hbm,
    out_ref,
    w_ref, blur_ref, cal_ref, today_ref,
    cur_in, arch, obs, stage, landed, gath, curr, dw, edge_lo, edge_hi, halo_up, halo_dn, season, parts, other, pack, packed,
    pieces, ends,
    local_sem, arch_sem, pair_sem, z_send, z_recv, y_send, y_recv, c_send, c_recv, h_send, h_recv, p_send, p_recv,
    r_send, r_recv, e_send, e_recv,
):
    date, tile = lax.axis_index("date"), lax.axis_index("tile")
    row, depth, core = date // 8, (date // 2) % 4, date % 2
    chip = row * 4 + depth
    tiles = 8

    def at(dy, dz):
        return ((((row + dy) % 4) * 4 + (depth + dz) % 4) * 2 + core, tile)

    def chip_at(dy, dz):
        return ((row + dy) % 4) * 4 + (depth + dz) % 4

    partner = (date + 1 - 2 * core, tile)
    others = [(dy, dz) for dy in range(4) for dz in range(4) if (dy, dz) != (0, 0)]

    load_cur = pltpu.make_async_copy(cur_hbm, cur_in, local_sem.at[0])
    load_cur.start()
    small = []
    for i, (src, dst) in enumerate(((w_hbm, w_ref), (blur_hbm, blur_ref), (cal_hbm, cal_ref), (today_hbm, today_ref))):
        copy = pltpu.make_async_copy(src, dst, local_sem.at[2 + i])
        copy.start()
        small.append(copy)
    barrier = pltpu.get_barrier_semaphore()
    for step in (1, 3, 2):
        pl.semaphore_signal(barrier, inc=1, device_id=at(0, step), device_id_type=MESH)
        pl.semaphore_signal(barrier, inc=1, device_id=at(step, 0), device_id_type=MESH)
    pl.semaphore_signal(barrier, inc=1, device_id=partner, device_id_type=MESH)

    @pl.when(tile > 0)
    def _():
        pl.semaphore_signal(barrier, inc=1, device_id=(date, tile - 1), device_id_type=MESH)

    @pl.when(tile < tiles - 1)
    def _():
        pl.semaphore_signal(barrier, inc=1, device_id=(date, tile + 1), device_id_type=MESH)

    loads = []
    for j, (t0, n, _) in enumerate(CHUNKS):
        copy = pltpu.make_async_copy(arch_hbm.at[:, pl.ds(t0, n)], arch.at[:, pl.ds(t0, n)], arch_sem.at[j])
        copy.start()
        loads.append(copy)
    load_obs = pltpu.make_async_copy(obs_hbm, obs, local_sem.at[1])
    load_obs.start()

    load_cur.wait()
    for x in range(4):
        for mine in range(2):
            cycle = core if mine else 1 - core
            values = cur_in[cycle, :, :, x, :].reshape(128, LEADS).T
            if mine:
                gath[:, row, depth, core * 4 + x, :] = values
            else:
                stage[:, x, :] = values

    pl.semaphore_wait(barrier, 7 + jnp.where(tile > 0, 1, 0) + jnp.where(tile < tiles - 1, 1, 0))

    pair = remote(stage, landed, pair_sem.at[0], pair_sem.at[1], partner)
    pair.start()

    zero = jnp.zeros((8, 128), jnp.float32)
    for k in range(REACH):
        for side in (k, LEADS + REACH + k):
            for i in range(8):
                dw[side, i] = zero
            halo_up[side] = zero
            halo_dn[side] = zero

    @pl.when(tile == 0)
    def _():
        for t in range(LEADS):
            halo_up[REACH + t] = zero

    @pl.when(tile == tiles - 1)
    def _():
        for t in range(LEADS):
            halo_dn[REACH + t] = zero

    for copy in small:
        copy.wait()
    sub = lax.broadcasted_iota(jnp.int32, (8, 128), 0)
    lane = lax.broadcasted_iota(jnp.int32, (8, 128), 1)
    days = jnp.zeros((8, 128), jnp.float32)
    for i in range(8):
        gap = (cal_ref[i % 4] - today_ref[i // 4]).astype(jnp.float32)
        days = jnp.where(sub == i, gap, days)
    season[...] = 0.5 * (1.0 - jnp.cos(2.0 * math.pi * days / 365.0))

    pair.wait_recv()
    for x in range(4):
        gath[:, row, depth, (1 - core) * 4 + x, :] = landed[:, x, :]

    def part(j, y, z):
        t0, n, _ = CHUNKS[j]
        return gath.at[pl.ds(t0, n), y, z]

    def first(j, d):
        mine = part(j, row, depth)
        to = at(d, 0) if CHUNKS[j][2] else at(0, d)
        return remote(mine, mine, z_send.at[j, d - 1], z_recv.at[j, d - 1], to)

    def first_wait(j, d):
        here = part(j, (row + 4 - d) % 4, depth) if CHUNKS[j][2] else part(j, row, (depth + 4 - d) % 4)
        remote(here, here, z_send.at[j, d - 1], z_recv.at[j, d - 1], partner).wait_recv()

    every = slice(None)
    halves = (pl.ds(0, 2), pl.ds(2, 2))

    def second(j, d):
        if CHUNKS[j][2]:
            t0, n, _ = CHUNKS[j]
            line = gath.at[pl.ds(t0, n), every, depth]
            return remote(line, line, y_send.at[j, d - 1], y_recv.at[j, d - 1], at(0, d))
        if d == 1 or d == 3:
            plane = part(j, row, every)
            return remote(plane, plane, y_send.at[j, d - 1], y_recv.at[j, d - 1], at(d, 0))
        raise ValueError(d)

    def second_wait(j, d):
        if CHUNKS[j][2]:
            t0, n, _ = CHUNKS[j]
            here = gath.at[pl.ds(t0, n), every, (depth + 4 - d) % 4]
        else:
            here = part(j, (row + 4 - d) % 4, every)
        remote(here, here, y_send.at[j, d - 1], y_recv.at[j, d - 1], partner).wait_recv()

    def forward(j, up):
        if up:
            half = part(j, (row + 3) % 4, halves[0])
            return remote(half, half, y_send.at[j, 1], y_recv.at[j, 1], at(1, 0))
        half = part(j, (row + 1) % 4, halves[1])
        return remote(half, half, y_send.at[j, 3], y_recv.at[j, 3], at(3, 0))

    def forward_wait(j, up):
        half = part(j, (row + 2) % 4, halves[0 if up else 1])
        sem = 1 if up else 3
        remote(half, half, y_send.at[j, sem], y_recv.at[j, sem], partner).wait_recv()

    def c_copy(j, cycle):
        t0, n, _ = CHUNKS[j]
        block = curr.at[cycle, pl.ds(t0, n)]
        return remote(block, block, c_send.at[j], c_recv.at[j], partner)

    def h_copy(j, up):
        t0, n, _ = CHUNKS[j]
        if up:
            return remote(
                edge_hi.at[pl.ds(t0, n)], halo_up.at[pl.ds(REACH + t0, n)], h_send.at[j, 0], h_recv.at[j, 0], (date, tile + 1)
            )
        return remote(
            edge_lo.at[pl.ds(t0, n)], halo_dn.at[pl.ds(REACH + t0, n)], h_send.at[j, 1], h_recv.at[j, 1], (date, tile - 1)
        )

    def p_copy(b):
        return remote(
            parts.at[1 - core, pl.ds(b * BLOCK, BLOCK)], other.at[pl.ds(b * BLOCK, BLOCK)], p_send.at[b], p_recv.at[b], partner
        )

    def r_copy(b, o):
        dy, dz = others[o]
        return remote(packed.at[b, chip_at(dy, dz)], pieces.at[b, o], r_send.at[b], r_recv.at[b], at(dy, dz))

    plain = [j for j in range(len(CHUNKS)) if not CHUNKS[j][2]]
    turned = [j for j in range(len(CHUNKS)) if CHUNKS[j][2]]
    for j in turned + plain:
        for d in (2, 1, 3):
            first(j, d).start()
    def relay(j):
        second_wait(j, 1)
        forward(j, True).start()
        second_wait(j, 3)
        forward(j, False).start()

    def onward(j):
        for d in (1, 3, 2):
            first_wait(j, d)
        for d in (2, 1, 3) if CHUNKS[j][2] else (1, 3):
            second(j, d).start()

    def transpose(j):
        t0, n, _ = CHUNKS[j]
        if CHUNKS[j][2]:
            for d in (1, 3, 2):
                second_wait(j, d)
        else:
            forward_wait(j, True)
            forward_wait(j, False)

        def turn(t, carry):
            curr[core, t] = gath[t].reshape(128, 128).T.reshape(16, 8, 128)
            return carry

        lax.fori_loop(t0, t0 + n, turn, 0)
        c_copy(j, core).start()

    def differences(j):
        t0, n, _ = CHUNKS[j]
        loads[j].wait()
        c_copy(j, 1 - core).wait_recv()

        def one(t, carry):
            for d in range(4):
                sums = [None, None]
                for p in range(16):
                    past = arch[d, t, p]
                    for c in range(2):
                        gap = curr[c, t, p] - past
                        term = gap * gap * w_ref[p]
                        sums[c] = term if p == 0 else sums[c] + term
                for c in range(2):
                    v = sums[c]
                    v = (
                        v
                        + jnp.where(lane > 0, pltpu.roll(v, 1, 1), 0.0)
                        + jnp.where(lane < 127, pltpu.roll(v, 127, 1), 0.0)
                    )
                    i = c * 4 + d
                    dw[t + REACH, i] = v
                    edge_lo[t, pl.ds(i, 1)] = v[0:1]
                    edge_hi[t, pl.ds(i, 1)] = v[7:8]
            return carry

        lax.fori_loop(t0, t0 + n, one, 0)

        @pl.when(tile < tiles - 1)
        def _():
            h_copy(j, True).start()

        @pl.when(tile > 0)
        def _():
            h_copy(j, False).start()

    scored, sent, seen = set(), [0], set()

    def scores(j):
        t0, n, _ = CHUNKS[j]
        if not seen:
            load_obs.wait()

        @pl.when(tile > 0)
        def _():
            h_copy(j, True).wait_recv()

        @pl.when(tile < tiles - 1)
        def _():
            h_copy(j, False).wait_recv()

        def one(t, carry):
            above, below = halo_up[t], halo_dn[t]
            for k in range(1, 2 * REACH + 1):
                above = above + halo_up[t + k]
                below = below + halo_dn[t + k]
            spread = blur_ref[t]
            inverse = 1.0 / jnp.full((8, 128), spread, jnp.float32)
            for c in range(2):
                dist = []
                for d in range(4):
                    i = c * 4 + d
                    v = dw[t, i]
                    for k in range(1, 2 * REACH + 1):
                        v = v + dw[t + k, i]
                    up = jnp.where(sub == 0, jnp.broadcast_to(above[i : i + 1], (8, 128)), pltpu.roll(v, 1, 0))
                    down = jnp.where(sub == 7, jnp.broadcast_to(below[i : i + 1], (8, 128)), pltpu.roll(v, 7, 0))
                    v = (v + up + down) * (1.0 / (16.0 * 9.0 * (2 * REACH + 1)))
                    dist.append(v + jnp.broadcast_to(season[pl.ds(i, 1)], (8, 128)))
                low = jnp.minimum(jnp.minimum(dist[0], dist[1]), jnp.minimum(dist[2], dist[3]))
                den = num = None
                for d in range(4):
                    e = jnp.exp((low - dist[d]) * inverse)
                    f = e * obs[d, t]
                    den = e if d == 0 else den + e
                    num = f if d == 0 else num + f
                parts[c, t, 0] = low - spread * jnp.log(den)
                parts[c, t, 1] = num / den
            return carry

        seen.update(range(t0, t0 + n))
        ready = [
            t for t in range(LEADS)
            if t not in scored and all(u in seen for u in range(max(t - REACH, 0), min(t + REACH + 1, LEADS)))
        ]
        while ready:
            stop = ready[0] + 1
            while stop in ready:
                stop += 1
            lax.fori_loop(ready[0], stop, one, 0)
            scored.update(range(ready[0], stop))
            ready = [t for t in ready if t >= stop]
        while sent[0] < BLOCKS and all(t in scored for t in range(sent[0] * BLOCK, (sent[0] + 1) * BLOCK)):
            p_copy(sent[0]).start()
            sent[0] += 1

    def combine(b):
        p_copy(b).wait_recv()

        def one(s, carry):
            t = b * BLOCK + s
            spread = blur_ref[t]
            a0, r0 = parts[core, t, 0], parts[core, t, 1]
            a1, r1 = other[t, 0], other[t, 1]
            low = jnp.minimum(a0, a1)
            e0, e1 = jnp.exp((low - a0) / spread), jnp.exp((low - a1) / spread)
            den = e0 + e1
            pack[0, :, s, :] = low - spread * jnp.log(den)
            pack[1, :, s, :] = (e0 * r0 + e1 * r1) / den
            return carry

        lax.fori_loop(0, BLOCK, one, 0)
        packed[b] = pack[...].reshape(128, 128).T.reshape(16, 8, 128)
        for o in range(15):
            r_copy(b, o).start()

    acts = {"F": onward, "R": relay, "T": transpose, "D": differences, "S": scores}
    combined = 0
    for kind, j in STEPS:
        due = sent[0]
        acts[kind](j)
        if kind != "R":
            while combined < due:
                combine(combined)
                combined += 1
    while combined < BLOCKS:
        combine(combined)
        combined += 1

    def e_copy(b, cycle):
        return remote(ends.at[cycle, b], ends.at[cycle, b], e_send.at[b], e_recv.at[b], partner)

    for b in range(BLOCKS):
        here = pieces.at[b]
        remote(here, here, r_send.at[b], r_recv.at[b], partner).wait_recv()
        spread = jnp.zeros((8, 128), jnp.float32)
        for s in range(BLOCK):
            spread = jnp.where(lane % BLOCK == s, blur_ref[b * BLOCK + s], spread)
        terms = [packed[b, chip]] + [pieces[b, o] for o in range(15)]
        low = functools.reduce(jnp.minimum, terms)
        den = num = None
        for i, v in enumerate(terms):
            e = jnp.exp((low - v) / spread)
            f = pltpu.roll(e, 64, 1) * v
            den = e if i == 0 else den + e
            num = f if i == 0 else num + f
        ends[core, b] = num / pltpu.roll(den, 64, 1)
        e_copy(b, core).start()

    for b in range(BLOCKS):
        e_copy(b, 1 - core).wait_recv()
    for c in range(2):
        blocks = []
        for b in range(BLOCKS):
            v = ends[c, b]
            blocks.append(jnp.where(core == 0, v, pltpu.roll(v, 4, 0)))
        for y in range(8):
            v = jnp.zeros((8, 128), jnp.float32)
            for b in range(BLOCKS):
                shift = (b * BLOCK - 64 - y * BLOCK) % 128
                moved = blocks[b] if shift == 0 else pltpu.roll(blocks[b], shift, 1)
                v = jnp.where(lane // BLOCK == b, moved, v)
            out_ref[c, y] = v[0:4, 0:LEADS]

    pair.wait_send()
    for j in range(len(CHUNKS)):
        for d in (1, 2, 3):
            first(j, d).wait_send()
            if CHUNKS[j][2] or d != 2:
                second(j, d).wait_send()
        if not CHUNKS[j][2]:
            forward(j, True).wait_send()
            forward(j, False).wait_send()
        c_copy(j, core).wait_send()

    @pl.when(tile < tiles - 1)
    def _():
        for j in range(len(CHUNKS)):
            h_copy(j, True).wait_send()

    @pl.when(tile > 0)
    def _():
        for j in range(len(CHUNKS)):
            h_copy(j, False).wait_send()

    for b in range(BLOCKS):
        p_copy(b).wait_send()
        e_copy(b, core).wait_send()
        here = pieces.at[b]
        remote(here, here, r_send.at[b], r_recv.at[b], partner).wait_send()


def local(current, archive, reports, weights, blur, calendar, today):
    count = len(CHUNKS)
    f32 = jnp.float32
    dma = pltpu.SemaphoreType.DMA
    leads = LEADS + 2 * REACH
    out = pl.pallas_call(
        kernel,
        out_shape=jax.ShapeDtypeStruct((2, 8, 4, LEADS), f32),
        in_specs=[pl.BlockSpec(memory_space=pl.ANY)] * 7,
        out_specs=pl.BlockSpec(memory_space=pltpu.VMEM),
        scratch_shapes=[
            pltpu.SMEM((16,), f32), pltpu.SMEM((LEADS,), f32), pltpu.SMEM((4,), jnp.int32), pltpu.SMEM((2,), jnp.int32),
            pltpu.VMEM((2, 16, 8, 4, LEADS), f32),
            pltpu.VMEM((4, LEADS, 16, 8, 128), f32),
            pltpu.VMEM((4, LEADS, 8, 128), f32),
            pltpu.VMEM((LEADS, 4, 128), f32),
            pltpu.VMEM((LEADS, 4, 128), f32),
            pltpu.VMEM((LEADS, 4, 4, 8, 128), f32),
            pltpu.VMEM((2, LEADS, 16, 8, 128), f32),
            pltpu.VMEM((leads, 8, 8, 128), f32),
            pltpu.VMEM((LEADS, 8, 128), f32),
            pltpu.VMEM((LEADS, 8, 128), f32),
            pltpu.VMEM((leads, 8, 128), f32),
            pltpu.VMEM((leads, 8, 128), f32),
            pltpu.VMEM((8, 128), f32),
            pltpu.VMEM((2, LEADS, 2, 8, 128), f32),
            pltpu.VMEM((LEADS, 2, 8, 128), f32),
            pltpu.VMEM((2, 8, BLOCK, 128), f32),
            pltpu.VMEM((BLOCKS, 16, 8, 128), f32),
            pltpu.VMEM((BLOCKS, 15, 8, 128), f32),
            pltpu.VMEM((2, BLOCKS, 8, 128), f32),
            dma((6,)),
            dma((count,)),
            dma((2,)),
            dma((count, 3)), dma((count, 3)),
            dma((count, 4)), dma((count, 4)),
            dma((count,)), dma((count,)),
            dma((count, 2)), dma((count, 2)),
            dma((BLOCKS,)), dma((BLOCKS,)),
            dma((BLOCKS,)), dma((BLOCKS,)),
            dma((BLOCKS,)), dma((BLOCKS,)),
        ],
        compiler_params=pltpu.CompilerParams(
            collective_id=0, has_side_effects=True, vmem_limit_bytes=60 * 2**20
        ),
    )(jnp.transpose(current, (0, 2, 3, 4, 1)), archive, reports, weights, blur, calendar, today)
    return jnp.transpose(out, (0, 3, 1, 2))


def solution(mesh):
    placed = (
        P(None, None, None, "tile", "date"),
        P("date", None, None, "tile", None),
        P("date", None, "tile", None),
        P(),
        P(),
        P("date"),
        P(),
    )
    return jax.shard_map(
        local, mesh=mesh, in_specs=placed, out_specs=P(None, None, "tile", "date"), check_vma=False
    )
```

```python
import functools
import math

import jax
import jax.numpy as jnp
from jax import lax
from jax.experimental import pallas as pl
from jax.experimental.pallas import tpu as pltpu
from jax.sharding import PartitionSpec as P

MESH = pl.DeviceIdType.MESH
LEADS = 24
REACH = 3
CHUNKS = ((6, 6, False, True), (12, 6, False, True), (18, 6, False, True), (0, 6, True, False))
STEPS = (
    ("F", 3), ("F", 0), ("F", 1), ("R", 0), ("F", 2), ("R", 1), ("T", 0), ("R", 2), ("T", 1), ("D", 0), ("T", 3), ("D", 1), ("T", 2), ("D", 3), ("S", 0), ("D", 2), ("S", 1), ("S", 3), ("S", 2),
)
BLOCK = 8
BLOCKS = LEADS // BLOCK


def remote(src, dst, send, recv, device):
    return pltpu.make_async_remote_copy(
        src_ref=src, dst_ref=dst, send_sem=send, recv_sem=recv, device_id=device, device_id_type=MESH
    )


def kernel(
    cur_hbm, arch_hbm, obs_hbm, w_hbm, blur_hbm, cal_hbm, today_hbm,
    out_ref,
    w_ref, blur_ref, cal_ref, today_ref,
    cur_in, arch, obs, stage, landed, gath, curr, dw, edge_lo, edge_hi, halo_up, halo_dn, season, parts, other, pack, packed,
    pieces, ends,
    local_sem, arch_sem, pair_sem, z_send, z_recv, y_send, y_recv, c_send, c_recv, h_send, h_recv, p_send, p_recv,
    r_send, r_recv, e_send, e_recv,
):
    date, tile = lax.axis_index("date"), lax.axis_index("tile")
    row, depth, core = date // 8, (date // 2) % 4, date % 2
    chip = row * 4 + depth
    tiles = 8

    def at(dy, dz):
        return ((((row + dy) % 4) * 4 + (depth + dz) % 4) * 2 + core, tile)

    def chip_at(dy, dz):
        return ((row + dy) % 4) * 4 + (depth + dz) % 4

    partner = (date + 1 - 2 * core, tile)
    others = [(dy, dz) for dy in range(4) for dz in range(4) if (dy, dz) != (0, 0)]

    load_cur = pltpu.make_async_copy(cur_hbm, cur_in, local_sem.at[0])
    load_cur.start()
    small = []
    for i, (src, dst) in enumerate(((w_hbm, w_ref), (blur_hbm, blur_ref), (cal_hbm, cal_ref), (today_hbm, today_ref))):
        copy = pltpu.make_async_copy(src, dst, local_sem.at[2 + i])
        copy.start()
        small.append(copy)
    barrier = pltpu.get_barrier_semaphore()
    for step in (1, 3, 2):
        pl.semaphore_signal(barrier, inc=1, device_id=at(0, step), device_id_type=MESH)
        pl.semaphore_signal(barrier, inc=1, device_id=at(step, 0), device_id_type=MESH)
    pl.semaphore_signal(barrier, inc=1, device_id=partner, device_id_type=MESH)

    @pl.when(tile > 0)
    def _():
        pl.semaphore_signal(barrier, inc=1, device_id=(date, tile - 1), device_id_type=MESH)

    @pl.when(tile < tiles - 1)
    def _():
        pl.semaphore_signal(barrier, inc=1, device_id=(date, tile + 1), device_id_type=MESH)

    loads = []
    for j, (t0, n, _, _) in enumerate(CHUNKS):
        copy = pltpu.make_async_copy(arch_hbm.at[:, pl.ds(t0, n)], arch.at[:, pl.ds(t0, n)], arch_sem.at[j])
        copy.start()
        loads.append(copy)
    load_obs = pltpu.make_async_copy(obs_hbm, obs, local_sem.at[1])
    load_obs.start()

    load_cur.wait()
    for x in range(4):
        for mine in range(2):
            cycle = core if mine else 1 - core
            values = cur_in[cycle, :, :, x, :].reshape(128, LEADS).T
            if mine:
                gath[:, row, depth, core * 4 + x, :] = values
            else:
                stage[:, x, :] = values

    pl.semaphore_wait(barrier, 7 + jnp.where(tile > 0, 1, 0) + jnp.where(tile < tiles - 1, 1, 0))

    pair = remote(stage, landed, pair_sem.at[0], pair_sem.at[1], partner)
    pair.start()

    zero = jnp.zeros((8, 128), jnp.float32)
    for k in range(REACH):
        for side in (k, LEADS + REACH + k):
            for i in range(8):
                dw[side, i] = zero
            halo_up[side] = zero
            halo_dn[side] = zero

    @pl.when(tile == 0)
    def _():
        for t in range(LEADS):
            halo_up[REACH + t] = zero

    @pl.when(tile == tiles - 1)
    def _():
        for t in range(LEADS):
            halo_dn[REACH + t] = zero

    for copy in small:
        copy.wait()
    sub = lax.broadcasted_iota(jnp.int32, (8, 128), 0)
    lane = lax.broadcasted_iota(jnp.int32, (8, 128), 1)
    days = jnp.zeros((8, 128), jnp.float32)
    for i in range(8):
        gap = (cal_ref[i % 4] - today_ref[i // 4]).astype(jnp.float32)
        days = jnp.where(sub == i, gap, days)
    season[...] = 0.5 * (1.0 - jnp.cos(2.0 * math.pi * days / 365.0))

    pair.wait_recv()
    for x in range(4):
        gath[:, row, depth, (1 - core) * 4 + x, :] = landed[:, x, :]

    def part(j, y, z):
        t0, n = CHUNKS[j][:2]
        return gath.at[pl.ds(t0, n), y, z]

    def first(j, d):
        mine = part(j, row, depth)
        to = at(d, 0) if CHUNKS[j][2] else at(0, d)
        return remote(mine, mine, z_send.at[j, d - 1], z_recv.at[j, d - 1], to)

    def first_wait(j, d):
        here = part(j, (row + 4 - d) % 4, depth) if CHUNKS[j][2] else part(j, row, (depth + 4 - d) % 4)
        remote(here, here, z_send.at[j, d - 1], z_recv.at[j, d - 1], partner).wait_recv()

    every = slice(None)
    halves = (pl.ds(0, 2), pl.ds(2, 2))

    def line(j, d, which):
        if CHUNKS[j][2]:
            return part(j, which, (depth + 4 - d) % 4)
        return part(j, (row + 4 - d) % 4, which)

    def ahead(j, d):
        return at(0, d) if CHUNKS[j][2] else at(d, 0)

    def second(j, d):
        mine = line(j, 0, every)
        return remote(mine, mine, y_send.at[j, d - 1], y_recv.at[j, d - 1], ahead(j, d))

    def second_wait(j, d):
        here = line(j, d, every)
        remote(here, here, y_send.at[j, d - 1], y_recv.at[j, d - 1], partner).wait_recv()

    def forward(j, up):
        half, sem = (line(j, 1, halves[0]), 1) if up else (line(j, 3, halves[1]), 3)
        return remote(half, half, y_send.at[j, sem], y_recv.at[j, sem], ahead(j, 1 if up else 3))

    def forward_wait(j, up):
        half, sem = (line(j, 2, halves[0]), 1) if up else (line(j, 2, halves[1]), 3)
        remote(half, half, y_send.at[j, sem], y_recv.at[j, sem], partner).wait_recv()

    def c_copy(j, cycle):
        t0, n = CHUNKS[j][:2]
        block = curr.at[cycle, pl.ds(t0, n)]
        return remote(block, block, c_send.at[j], c_recv.at[j], partner)

    def h_copy(j, up):
        t0, n = CHUNKS[j][:2]
        if up:
            return remote(
                edge_hi.at[pl.ds(t0, n)], halo_up.at[pl.ds(REACH + t0, n)], h_send.at[j, 0], h_recv.at[j, 0], (date, tile + 1)
            )
        return remote(
            edge_lo.at[pl.ds(t0, n)], halo_dn.at[pl.ds(REACH + t0, n)], h_send.at[j, 1], h_recv.at[j, 1], (date, tile - 1)
        )

    def p_copy(b):
        return remote(
            parts.at[1 - core, pl.ds(b * BLOCK, BLOCK)], other.at[pl.ds(b * BLOCK, BLOCK)], p_send.at[b], p_recv.at[b], partner
        )

    def r_copy(b, o):
        dy, dz = others[o]
        return remote(packed.at[b, chip_at(dy, dz)], pieces.at[b, o], r_send.at[b], r_recv.at[b], at(dy, dz))

    plain = [j for j in range(len(CHUNKS)) if not CHUNKS[j][2]]
    turned = [j for j in range(len(CHUNKS)) if CHUNKS[j][2]]
    for j in turned + plain:
        for d in (2, 1, 3):
            first(j, d).start()
    def relay(j):
        second_wait(j, 1)
        forward(j, True).start()
        second_wait(j, 3)
        forward(j, False).start()

    def onward(j):
        for d in (1, 3, 2):
            first_wait(j, d)
        for d in (1, 3) if CHUNKS[j][3] else (2, 1, 3):
            second(j, d).start()

    def transpose(j):
        t0, n = CHUNKS[j][:2]
        if not CHUNKS[j][3]:
            for d in (1, 3, 2):
                second_wait(j, d)
        else:
            forward_wait(j, True)
            forward_wait(j, False)

        def turn(t, carry):
            curr[core, t] = gath[t].reshape(128, 128).T.reshape(16, 8, 128)
            return carry

        lax.fori_loop(t0, t0 + n, turn, 0, unroll=True)
        c_copy(j, core).start()

    def differences(j):
        t0, n = CHUNKS[j][:2]
        loads[j].wait()
        c_copy(j, 1 - core).wait_recv()

        def one(t, carry):
            sums = {}
            for p in range(16):
                now = curr[0, t, p], curr[1, t, p]
                for d in range(4):
                    past = arch[d, t, p]
                    for c in range(2):
                        gap = now[c] - past
                        term = gap * gap * w_ref[p]
                        sums[c, d] = term if p == 0 else sums[c, d] + term
            for d in range(4):
                for c in range(2):
                    v = sums[c, d]
                    v = (
                        v
                        + jnp.where(lane > 0, pltpu.roll(v, 1, 1), 0.0)
                        + jnp.where(lane < 127, pltpu.roll(v, 127, 1), 0.0)
                    )
                    i = c * 4 + d
                    dw[t + REACH, i] = v
                    edge_lo[t, pl.ds(i, 1)] = v[0:1]
                    edge_hi[t, pl.ds(i, 1)] = v[7:8]
            return carry

        lax.fori_loop(t0, t0 + n, one, 0)

        @pl.when(tile < tiles - 1)
        def _():
            h_copy(j, True).start()

        @pl.when(tile > 0)
        def _():
            h_copy(j, False).start()

    scored, sent, seen = set(), [0], set()

    def scores(j):
        t0, n = CHUNKS[j][:2]
        if not seen:
            load_obs.wait()

        @pl.when(tile > 0)
        def _():
            h_copy(j, True).wait_recv()

        @pl.when(tile < tiles - 1)
        def _():
            h_copy(j, False).wait_recv()

        def one(t, carry):
            above, below = halo_up[t], halo_dn[t]
            for k in range(1, 2 * REACH + 1):
                above = above + halo_up[t + k]
                below = below + halo_dn[t + k]
            spread = blur_ref[t]
            inverse = 1.0 / jnp.full((8, 128), spread, jnp.float32)
            for c in range(2):
                dist = []
                for d in range(4):
                    i = c * 4 + d
                    v = dw[t, i]
                    for k in range(1, 2 * REACH + 1):
                        v = v + dw[t + k, i]
                    up = jnp.where(sub == 0, jnp.broadcast_to(above[i : i + 1], (8, 128)), pltpu.roll(v, 1, 0))
                    down = jnp.where(sub == 7, jnp.broadcast_to(below[i : i + 1], (8, 128)), pltpu.roll(v, 7, 0))
                    v = (v + up + down) * (1.0 / (16.0 * 9.0 * (2 * REACH + 1)))
                    dist.append(v + jnp.broadcast_to(season[pl.ds(i, 1)], (8, 128)))
                low = jnp.minimum(jnp.minimum(dist[0], dist[1]), jnp.minimum(dist[2], dist[3]))
                den = num = None
                for d in range(4):
                    e = jnp.exp((low - dist[d]) * inverse)
                    f = e * obs[d, t]
                    den = e if d == 0 else den + e
                    num = f if d == 0 else num + f
                parts[c, t, 0] = low - spread * jnp.log(den)
                parts[c, t, 1] = num / den
            return carry

        seen.update(range(t0, t0 + n))
        ready = [
            t for t in range(LEADS)
            if t not in scored and all(u in seen for u in range(max(t - REACH, 0), min(t + REACH + 1, LEADS)))
        ]
        while ready:
            stop = ready[0] + 1
            while stop in ready:
                stop += 1
            lax.fori_loop(ready[0], stop, one, 0, unroll=2)
            scored.update(range(ready[0], stop))
            ready = [t for t in ready if t >= stop]
        while sent[0] < BLOCKS and all(t in scored for t in range(sent[0] * BLOCK, (sent[0] + 1) * BLOCK)):
            p_copy(sent[0]).start()
            sent[0] += 1

    def combine(b):
        p_copy(b).wait_recv()

        def one(s, carry):
            t = b * BLOCK + s
            spread = blur_ref[t]
            a0, r0 = parts[core, t, 0], parts[core, t, 1]
            a1, r1 = other[t, 0], other[t, 1]
            low = jnp.minimum(a0, a1)
            e0, e1 = jnp.exp((low - a0) / spread), jnp.exp((low - a1) / spread)
            den = e0 + e1
            pack[0, :, s, :] = low - spread * jnp.log(den)
            pack[1, :, s, :] = (e0 * r0 + e1 * r1) / den
            return carry

        lax.fori_loop(0, BLOCK, one, 0, unroll=True)
        packed[b] = pack[...].reshape(128, 128).T.reshape(16, 8, 128)
        for o in range(15):
            r_copy(b, o).start()

    acts = {"F": onward, "R": relay, "T": transpose, "D": differences, "S": scores}
    combined = 0
    for kind, j in STEPS:
        due = sent[0]
        acts[kind](j)
        if kind != "R":
            while combined < due:
                combine(combined)
                combined += 1
    while combined < BLOCKS:
        combine(combined)
        combined += 1

    def e_copy(b, cycle):
        return remote(ends.at[cycle, b], ends.at[cycle, b], e_send.at[b], e_recv.at[b], partner)

    for b in range(BLOCKS):
        here = pieces.at[b]
        remote(here, here, r_send.at[b], r_recv.at[b], partner).wait_recv()
        spread = jnp.zeros((8, 128), jnp.float32)
        for s in range(BLOCK):
            spread = jnp.where(lane % BLOCK == s, blur_ref[b * BLOCK + s], spread)
        terms = [packed[b, chip]] + [pieces[b, o] for o in range(15)]
        low = functools.reduce(jnp.minimum, terms)
        den = num = None
        for i, v in enumerate(terms):
            e = jnp.exp((low - v) / spread)
            f = pltpu.roll(e, 64, 1) * v
            den = e if i == 0 else den + e
            num = f if i == 0 else num + f
        ends[core, b] = num / pltpu.roll(den, 64, 1)
        e_copy(b, core).start()

    for b in range(BLOCKS):
        e_copy(b, 1 - core).wait_recv()
    for c in range(2):
        blocks = []
        for b in range(BLOCKS):
            v = ends[c, b]
            blocks.append(jnp.where(core == 0, v, pltpu.roll(v, 4, 0)))
        for y in range(8):
            v = jnp.zeros((8, 128), jnp.float32)
            for b in range(BLOCKS):
                shift = (b * BLOCK - 64 - y * BLOCK) % 128
                moved = blocks[b] if shift == 0 else pltpu.roll(blocks[b], shift, 1)
                v = jnp.where(lane // BLOCK == b, moved, v)
            out_ref[c, y] = v[0:4, 0:LEADS]

    pair.wait_send()
    for j in range(len(CHUNKS)):
        for d in (1, 2, 3):
            first(j, d).wait_send()
            if d != 2 or not CHUNKS[j][3]:
                second(j, d).wait_send()
        if CHUNKS[j][3]:
            forward(j, True).wait_send()
            forward(j, False).wait_send()
        c_copy(j, core).wait_send()

    @pl.when(tile < tiles - 1)
    def _():
        for j in range(len(CHUNKS)):
            h_copy(j, True).wait_send()

    @pl.when(tile > 0)
    def _():
        for j in range(len(CHUNKS)):
            h_copy(j, False).wait_send()

    for b in range(BLOCKS):
        p_copy(b).wait_send()
        e_copy(b, core).wait_send()
        here = pieces.at[b]
        remote(here, here, r_send.at[b], r_recv.at[b], partner).wait_send()


def local(current, archive, reports, weights, blur, calendar, today):
    count = len(CHUNKS)
    f32 = jnp.float32
    dma = pltpu.SemaphoreType.DMA
    leads = LEADS + 2 * REACH
    out = pl.pallas_call(
        kernel,
        out_shape=jax.ShapeDtypeStruct((2, 8, 4, LEADS), f32),
        in_specs=[pl.BlockSpec(memory_space=pl.ANY)] * 7,
        out_specs=pl.BlockSpec(memory_space=pltpu.VMEM),
        scratch_shapes=[
            pltpu.SMEM((16,), f32), pltpu.SMEM((LEADS,), f32), pltpu.SMEM((4,), jnp.int32), pltpu.SMEM((2,), jnp.int32),
            pltpu.VMEM((2, 16, 8, 4, LEADS), f32),
            pltpu.VMEM((4, LEADS, 16, 8, 128), f32),
            pltpu.VMEM((4, LEADS, 8, 128), f32),
            pltpu.VMEM((LEADS, 4, 128), f32),
            pltpu.VMEM((LEADS, 4, 128), f32),
            pltpu.VMEM((LEADS, 4, 4, 8, 128), f32),
            pltpu.VMEM((2, LEADS, 16, 8, 128), f32),
            pltpu.VMEM((leads, 8, 8, 128), f32),
            pltpu.VMEM((LEADS, 8, 128), f32),
            pltpu.VMEM((LEADS, 8, 128), f32),
            pltpu.VMEM((leads, 8, 128), f32),
            pltpu.VMEM((leads, 8, 128), f32),
            pltpu.VMEM((8, 128), f32),
            pltpu.VMEM((2, LEADS, 2, 8, 128), f32),
            pltpu.VMEM((LEADS, 2, 8, 128), f32),
            pltpu.VMEM((2, 8, BLOCK, 128), f32),
            pltpu.VMEM((BLOCKS, 16, 8, 128), f32),
            pltpu.VMEM((BLOCKS, 15, 8, 128), f32),
            pltpu.VMEM((2, BLOCKS, 8, 128), f32),
            dma((6,)),
            dma((count,)),
            dma((2,)),
            dma((count, 3)), dma((count, 3)),
            dma((count, 4)), dma((count, 4)),
            dma((count,)), dma((count,)),
            dma((count, 2)), dma((count, 2)),
            dma((BLOCKS,)), dma((BLOCKS,)),
            dma((BLOCKS,)), dma((BLOCKS,)),
            dma((BLOCKS,)), dma((BLOCKS,)),
        ],
        compiler_params=pltpu.CompilerParams(
            collective_id=0, has_side_effects=True, vmem_limit_bytes=60 * 2**20
        ),
    )(jnp.transpose(current, (0, 2, 3, 4, 1)), archive, reports, weights, blur, calendar, today)
    return jnp.transpose(out, (0, 3, 1, 2))


def solution(mesh):
    placed = (
        P(None, None, None, "tile", "date"),
        P("date", None, None, "tile", None),
        P("date", None, "tile", None),
        P(),
        P(),
        P("date"),
        P(),
    )
    return jax.shard_map(
        local, mesh=mesh, in_specs=placed, out_specs=P(None, None, "tile", "date"), check_vma=False
    )
```

```python
import functools
import math

import jax
import jax.numpy as jnp
from jax import lax
from jax.experimental import pallas as pl
from jax.experimental.pallas import tpu as pltpu
from jax.sharding import PartitionSpec as P

MESH = pl.DeviceIdType.MESH
LEADS = 24
REACH = 3
CHUNKS = ((6, 7, False, True), (13, 7, False, True), (20, 4, False, True), (0, 6, True, False))
STEPS = (
    ("F", 3), ("F", 0), ("F", 1), ("R", 0), ("F", 2), ("R", 1), ("T", 0), ("R", 2), ("T", 1), ("D", 0), ("T", 3), ("D", 1), ("T", 2), ("D", 3), ("S", 0), ("D", 2), ("S", 1), ("S", 3), ("S", 2),
)
BLOCK = 8
BLOCKS = LEADS // BLOCK


def remote(src, dst, send, recv, device):
    return pltpu.make_async_remote_copy(
        src_ref=src, dst_ref=dst, send_sem=send, recv_sem=recv, device_id=device, device_id_type=MESH
    )


def kernel(
    cur_hbm, arch_hbm, obs_hbm, w_hbm, blur_hbm, cal_hbm, today_hbm,
    out_ref,
    w_ref, blur_ref, cal_ref, today_ref,
    cur_in, arch, obs, stage, landed, gath, curr, dw, edge_lo, edge_hi, halo_up, halo_dn, season, parts, other, pack, packed,
    pieces, ends,
    local_sem, arch_sem, pair_sem, z_send, z_recv, y_send, y_recv, c_send, c_recv, h_send, h_recv, p_send, p_recv,
    r_send, r_recv, e_send, e_recv,
):
    date, tile = lax.axis_index("date"), lax.axis_index("tile")
    row, depth, core = date // 8, (date // 2) % 4, date % 2
    chip = row * 4 + depth
    tiles = 8

    def at(dy, dz):
        return ((((row + dy) % 4) * 4 + (depth + dz) % 4) * 2 + core, tile)

    def chip_at(dy, dz):
        return ((row + dy) % 4) * 4 + (depth + dz) % 4

    partner = (date + 1 - 2 * core, tile)
    others = [(dy, dz) for dy in range(4) for dz in range(4) if (dy, dz) != (0, 0)]

    load_cur = pltpu.make_async_copy(cur_hbm, cur_in, local_sem.at[0])
    load_cur.start()
    small = []
    for i, (src, dst) in enumerate(((w_hbm, w_ref), (blur_hbm, blur_ref), (cal_hbm, cal_ref), (today_hbm, today_ref))):
        copy = pltpu.make_async_copy(src, dst, local_sem.at[2 + i])
        copy.start()
        small.append(copy)
    barrier = pltpu.get_barrier_semaphore()
    for step in (1, 3, 2):
        pl.semaphore_signal(barrier, inc=1, device_id=at(0, step), device_id_type=MESH)
        pl.semaphore_signal(barrier, inc=1, device_id=at(step, 0), device_id_type=MESH)
    pl.semaphore_signal(barrier, inc=1, device_id=partner, device_id_type=MESH)

    @pl.when(tile > 0)
    def _():
        pl.semaphore_signal(barrier, inc=1, device_id=(date, tile - 1), device_id_type=MESH)

    @pl.when(tile < tiles - 1)
    def _():
        pl.semaphore_signal(barrier, inc=1, device_id=(date, tile + 1), device_id_type=MESH)

    loads = []
    for j, (t0, n, _, _) in enumerate(CHUNKS):
        copy = pltpu.make_async_copy(arch_hbm.at[:, pl.ds(t0, n)], arch.at[:, pl.ds(t0, n)], arch_sem.at[j])
        copy.start()
        loads.append(copy)
    load_obs = pltpu.make_async_copy(obs_hbm, obs, local_sem.at[1])
    load_obs.start()

    load_cur.wait()
    for x in range(4):
        for mine in range(2):
            cycle = core if mine else 1 - core
            values = cur_in[cycle, :, :, x, :].reshape(128, LEADS).T
            if mine:
                gath[:, row, depth, core * 4 + x, :] = values
            else:
                stage[:, x, :] = values

    pl.semaphore_wait(barrier, 7 + jnp.where(tile > 0, 1, 0) + jnp.where(tile < tiles - 1, 1, 0))

    pair = remote(stage, landed, pair_sem.at[0], pair_sem.at[1], partner)
    pair.start()

    zero = jnp.zeros((8, 128), jnp.float32)
    for k in range(REACH):
        for side in (k, LEADS + REACH + k):
            for i in range(8):
                dw[side, i] = zero
            halo_up[side] = zero
            halo_dn[side] = zero

    @pl.when(tile == 0)
    def _():
        for t in range(LEADS):
            halo_up[REACH + t] = zero

    @pl.when(tile == tiles - 1)
    def _():
        for t in range(LEADS):
            halo_dn[REACH + t] = zero

    for copy in small:
        copy.wait()
    sub = lax.broadcasted_iota(jnp.int32, (8, 128), 0)
    lane = lax.broadcasted_iota(jnp.int32, (8, 128), 1)
    days = jnp.zeros((8, 128), jnp.float32)
    for i in range(8):
        gap = (cal_ref[i % 4] - today_ref[i // 4]).astype(jnp.float32)
        days = jnp.where(sub == i, gap, days)
    season[...] = 0.5 * (1.0 - jnp.cos(2.0 * math.pi * days / 365.0))

    pair.wait_recv()
    for x in range(4):
        gath[:, row, depth, (1 - core) * 4 + x, :] = landed[:, x, :]

    def part(j, y, z):
        t0, n = CHUNKS[j][:2]
        return gath.at[pl.ds(t0, n), y, z]

    def first(j, d):
        mine = part(j, row, depth)
        to = at(d, 0) if CHUNKS[j][2] else at(0, d)
        return remote(mine, mine, z_send.at[j, d - 1], z_recv.at[j, d - 1], to)

    def first_wait(j, d):
        here = part(j, (row + 4 - d) % 4, depth) if CHUNKS[j][2] else part(j, row, (depth + 4 - d) % 4)
        remote(here, here, z_send.at[j, d - 1], z_recv.at[j, d - 1], partner).wait_recv()

    every = slice(None)
    halves = (pl.ds(0, 2), pl.ds(2, 2))

    def line(j, d, which):
        if CHUNKS[j][2]:
            return part(j, which, (depth + 4 - d) % 4)
        return part(j, (row + 4 - d) % 4, which)

    def ahead(j, d):
        return at(0, d) if CHUNKS[j][2] else at(d, 0)

    def second(j, d):
        mine = line(j, 0, every)
        return remote(mine, mine, y_send.at[j, d - 1], y_recv.at[j, d - 1], ahead(j, d))

    def second_wait(j, d):
        here = line(j, d, every)
        remote(here, here, y_send.at[j, d - 1], y_recv.at[j, d - 1], partner).wait_recv()

    def forward(j, up):
        half, sem = (line(j, 1, halves[0]), 1) if up else (line(j, 3, halves[1]), 3)
        return remote(half, half, y_send.at[j, sem], y_recv.at[j, sem], ahead(j, 1 if up else 3))

    def forward_wait(j, up):
        half, sem = (line(j, 2, halves[0]), 1) if up else (line(j, 2, halves[1]), 3)
        remote(half, half, y_send.at[j, sem], y_recv.at[j, sem], partner).wait_recv()

    def c_copy(j, cycle):
        t0, n = CHUNKS[j][:2]
        block = curr.at[cycle, pl.ds(t0, n)]
        return remote(block, block, c_send.at[j], c_recv.at[j], partner)

    def h_copy(j, up):
        t0, n = CHUNKS[j][:2]
        if up:
            return remote(
                edge_hi.at[pl.ds(t0, n)], halo_up.at[pl.ds(REACH + t0, n)], h_send.at[j, 0], h_recv.at[j, 0], (date, tile + 1)
            )
        return remote(
            edge_lo.at[pl.ds(t0, n)], halo_dn.at[pl.ds(REACH + t0, n)], h_send.at[j, 1], h_recv.at[j, 1], (date, tile - 1)
        )

    def p_copy(b):
        return remote(
            parts.at[1 - core, pl.ds(b * BLOCK, BLOCK)], other.at[pl.ds(b * BLOCK, BLOCK)], p_send.at[b], p_recv.at[b], partner
        )

    def r_copy(b, o):
        dy, dz = others[o]
        return remote(packed.at[b, chip_at(dy, dz)], pieces.at[b, o], r_send.at[b], r_recv.at[b], at(dy, dz))

    plain = [j for j in range(len(CHUNKS)) if not CHUNKS[j][2]]
    turned = [j for j in range(len(CHUNKS)) if CHUNKS[j][2]]
    for j in turned + plain:
        for d in (2, 1, 3):
            first(j, d).start()
    def relay(j):
        second_wait(j, 1)
        forward(j, True).start()
        second_wait(j, 3)
        forward(j, False).start()

    def onward(j):
        for d in (1, 3, 2):
            first_wait(j, d)
        for d in (1, 3) if CHUNKS[j][3] else (2, 1, 3):
            second(j, d).start()

    def transpose(j):
        t0, n = CHUNKS[j][:2]
        if not CHUNKS[j][3]:
            for d in (1, 3, 2):
                second_wait(j, d)
        else:
            forward_wait(j, True)
            forward_wait(j, False)

        def turn(t, carry):
            curr[core, t] = gath[t].reshape(128, 128).T.reshape(16, 8, 128)
            return carry

        lax.fori_loop(t0, t0 + n, turn, 0, unroll=True)
        c_copy(j, core).start()

    def differences(j):
        t0, n = CHUNKS[j][:2]
        loads[j].wait()
        c_copy(j, 1 - core).wait_recv()

        def one(t, carry):
            sums = {}
            for p in range(16):
                now = curr[0, t, p], curr[1, t, p]
                for d in range(4):
                    past = arch[d, t, p]
                    for c in range(2):
                        gap = now[c] - past
                        term = gap * gap * w_ref[p]
                        sums[c, d] = term if p == 0 else sums[c, d] + term
            for d in range(4):
                for c in range(2):
                    v = sums[c, d]
                    v = (
                        v
                        + jnp.where(lane > 0, pltpu.roll(v, 1, 1), 0.0)
                        + jnp.where(lane < 127, pltpu.roll(v, 127, 1), 0.0)
                    )
                    i = c * 4 + d
                    dw[t + REACH, i] = v
                    edge_lo[t, pl.ds(i, 1)] = v[0:1]
                    edge_hi[t, pl.ds(i, 1)] = v[7:8]
            return carry

        lax.fori_loop(t0, t0 + n, one, 0)

        @pl.when(tile < tiles - 1)
        def _():
            h_copy(j, True).start()

        @pl.when(tile > 0)
        def _():
            h_copy(j, False).start()

    scored, sent, seen = set(), [0], set()

    def scores(j):
        t0, n = CHUNKS[j][:2]
        if not seen:
            load_obs.wait()

        @pl.when(tile > 0)
        def _():
            h_copy(j, True).wait_recv()

        @pl.when(tile < tiles - 1)
        def _():
            h_copy(j, False).wait_recv()

        def one(t, carry):
            above, below = halo_up[t], halo_dn[t]
            for k in range(1, 2 * REACH + 1):
                above = above + halo_up[t + k]
                below = below + halo_dn[t + k]
            spread = blur_ref[t]
            inverse = 1.0 / jnp.full((8, 128), spread, jnp.float32)
            for c in range(2):
                dist = []
                for d in range(4):
                    i = c * 4 + d
                    v = dw[t, i]
                    for k in range(1, 2 * REACH + 1):
                        v = v + dw[t + k, i]
                    up = jnp.where(sub == 0, jnp.broadcast_to(above[i : i + 1], (8, 128)), pltpu.roll(v, 1, 0))
                    down = jnp.where(sub == 7, jnp.broadcast_to(below[i : i + 1], (8, 128)), pltpu.roll(v, 7, 0))
                    v = (v + up + down) * (1.0 / (16.0 * 9.0 * (2 * REACH + 1)))
                    dist.append(v + jnp.broadcast_to(season[pl.ds(i, 1)], (8, 128)))
                low = jnp.minimum(jnp.minimum(dist[0], dist[1]), jnp.minimum(dist[2], dist[3]))
                den = num = None
                for d in range(4):
                    e = jnp.exp((low - dist[d]) * inverse)
                    f = e * obs[d, t]
                    den = e if d == 0 else den + e
                    num = f if d == 0 else num + f
                parts[c, t, 0] = low - spread * jnp.log(den)
                parts[c, t, 1] = num / den
            return carry

        seen.update(range(t0, t0 + n))
        ready = [
            t for t in range(LEADS)
            if t not in scored and all(u in seen for u in range(max(t - REACH, 0), min(t + REACH + 1, LEADS)))
        ]
        while ready:
            stop = ready[0] + 1
            while stop in ready:
                stop += 1
            lax.fori_loop(ready[0], stop, one, 0, unroll=2)
            scored.update(range(ready[0], stop))
            ready = [t for t in ready if t >= stop]
        while sent[0] < BLOCKS and all(t in scored for t in range(sent[0] * BLOCK, (sent[0] + 1) * BLOCK)):
            p_copy(sent[0]).start()
            sent[0] += 1

    def combine(b):
        p_copy(b).wait_recv()

        def one(s, carry):
            t = b * BLOCK + s
            spread = blur_ref[t]
            a0, r0 = parts[core, t, 0], parts[core, t, 1]
            a1, r1 = other[t, 0], other[t, 1]
            low = jnp.minimum(a0, a1)
            e0, e1 = jnp.exp((low - a0) / spread), jnp.exp((low - a1) / spread)
            den = e0 + e1
            pack[0, :, s, :] = low - spread * jnp.log(den)
            pack[1, :, s, :] = (e0 * r0 + e1 * r1) / den
            return carry

        lax.fori_loop(0, BLOCK, one, 0, unroll=True)
        packed[b] = pack[...].reshape(128, 128).T.reshape(16, 8, 128)
        for o in range(15):
            r_copy(b, o).start()

    acts = {"F": onward, "R": relay, "T": transpose, "D": differences, "S": scores}
    combined = 0
    for kind, j in STEPS:
        due = sent[0]
        acts[kind](j)
        if kind != "R":
            while combined < due:
                combine(combined)
                combined += 1
    while combined < BLOCKS:
        combine(combined)
        combined += 1

    def e_copy(b, cycle):
        return remote(ends.at[cycle, b], ends.at[cycle, b], e_send.at[b], e_recv.at[b], partner)

    for b in range(BLOCKS):
        here = pieces.at[b]
        remote(here, here, r_send.at[b], r_recv.at[b], partner).wait_recv()
        spread = jnp.zeros((8, 128), jnp.float32)
        for s in range(BLOCK):
            spread = jnp.where(lane % BLOCK == s, blur_ref[b * BLOCK + s], spread)
        terms = [packed[b, chip]] + [pieces[b, o] for o in range(15)]
        low = functools.reduce(jnp.minimum, terms)
        den = num = None
        for i, v in enumerate(terms):
            e = jnp.exp((low - v) / spread)
            f = pltpu.roll(e, 64, 1) * v
            den = e if i == 0 else den + e
            num = f if i == 0 else num + f
        ends[core, b] = num / pltpu.roll(den, 64, 1)
        e_copy(b, core).start()

    for b in range(BLOCKS):
        e_copy(b, 1 - core).wait_recv()
    for c in range(2):
        blocks = []
        for b in range(BLOCKS):
            v = ends[c, b]
            blocks.append(jnp.where(core == 0, v, pltpu.roll(v, 4, 0)))
        for y in range(8):
            v = jnp.zeros((8, 128), jnp.float32)
            for b in range(BLOCKS):
                shift = (b * BLOCK - 64 - y * BLOCK) % 128
                moved = blocks[b] if shift == 0 else pltpu.roll(blocks[b], shift, 1)
                v = jnp.where(lane // BLOCK == b, moved, v)
            out_ref[c, y] = v[0:4, 0:LEADS]

    pair.wait_send()
    for j in range(len(CHUNKS)):
        for d in (1, 2, 3):
            first(j, d).wait_send()
            if d != 2 or not CHUNKS[j][3]:
                second(j, d).wait_send()
        if CHUNKS[j][3]:
            forward(j, True).wait_send()
            forward(j, False).wait_send()
        c_copy(j, core).wait_send()

    @pl.when(tile < tiles - 1)
    def _():
        for j in range(len(CHUNKS)):
            h_copy(j, True).wait_send()

    @pl.when(tile > 0)
    def _():
        for j in range(len(CHUNKS)):
            h_copy(j, False).wait_send()

    for b in range(BLOCKS):
        p_copy(b).wait_send()
        e_copy(b, core).wait_send()
        here = pieces.at[b]
        remote(here, here, r_send.at[b], r_recv.at[b], partner).wait_send()


def local(current, archive, reports, weights, blur, calendar, today):
    count = len(CHUNKS)
    f32 = jnp.float32
    dma = pltpu.SemaphoreType.DMA
    leads = LEADS + 2 * REACH
    out = pl.pallas_call(
        kernel,
        out_shape=jax.ShapeDtypeStruct((2, 8, 4, LEADS), f32),
        in_specs=[pl.BlockSpec(memory_space=pl.ANY)] * 7,
        out_specs=pl.BlockSpec(memory_space=pltpu.VMEM),
        scratch_shapes=[
            pltpu.SMEM((16,), f32), pltpu.SMEM((LEADS,), f32), pltpu.SMEM((4,), jnp.int32), pltpu.SMEM((2,), jnp.int32),
            pltpu.VMEM((2, 16, 8, 4, LEADS), f32),
            pltpu.VMEM((4, LEADS, 16, 8, 128), f32),
            pltpu.VMEM((4, LEADS, 8, 128), f32),
            pltpu.VMEM((LEADS, 4, 128), f32),
            pltpu.VMEM((LEADS, 4, 128), f32),
            pltpu.VMEM((LEADS, 4, 4, 8, 128), f32),
            pltpu.VMEM((2, LEADS, 16, 8, 128), f32),
            pltpu.VMEM((leads, 8, 8, 128), f32),
            pltpu.VMEM((LEADS, 8, 128), f32),
            pltpu.VMEM((LEADS, 8, 128), f32),
            pltpu.VMEM((leads, 8, 128), f32),
            pltpu.VMEM((leads, 8, 128), f32),
            pltpu.VMEM((8, 128), f32),
            pltpu.VMEM((2, LEADS, 2, 8, 128), f32),
            pltpu.VMEM((LEADS, 2, 8, 128), f32),
            pltpu.VMEM((2, 8, BLOCK, 128), f32),
            pltpu.VMEM((BLOCKS, 16, 8, 128), f32),
            pltpu.VMEM((BLOCKS, 15, 8, 128), f32),
            pltpu.VMEM((2, BLOCKS, 8, 128), f32),
            dma((6,)),
            dma((count,)),
            dma((2,)),
            dma((count, 3)), dma((count, 3)),
            dma((count, 4)), dma((count, 4)),
            dma((count,)), dma((count,)),
            dma((count, 2)), dma((count, 2)),
            dma((BLOCKS,)), dma((BLOCKS,)),
            dma((BLOCKS,)), dma((BLOCKS,)),
            dma((BLOCKS,)), dma((BLOCKS,)),
        ],
        compiler_params=pltpu.CompilerParams(
            collective_id=0, has_side_effects=True, vmem_limit_bytes=60 * 2**20
        ),
    )(jnp.transpose(current, (0, 2, 3, 4, 1)), archive, reports, weights, blur, calendar, today)
    return jnp.transpose(out, (0, 3, 1, 2))


def solution(mesh):
    placed = (
        P(None, None, None, "tile", "date"),
        P("date", None, None, "tile", None),
        P("date", None, "tile", None),
        P(),
        P(),
        P("date"),
        P(),
    )
    return jax.shard_map(
        local, mesh=mesh, in_specs=placed, out_specs=P(None, None, "tile", "date"), check_vma=False
    )
```

```python
import functools
import math

import jax
import jax.numpy as jnp
from jax import lax
from jax.experimental import pallas as pl
from jax.experimental.pallas import tpu as pltpu
from jax.sharding import PartitionSpec as P

MESH = pl.DeviceIdType.MESH
LEADS = 24
REACH = 3
CHUNKS = ((6, 7, False, True), (13, 7, False, True), (20, 4, False, True), (0, 6, True, False))
STEPS = (
    ("F", 3), ("F", 0), ("F", 1), ("R", 0), ("F", 2), ("R", 1), ("T", 0), ("R", 2), ("T", 1), ("D", 0), ("T", 3), ("D", 1), ("T", 2), ("D", 3), ("D", 2), ("S", 0), ("S", 1), ("S", 3), ("S", 2),
)
BLOCK = 8
BLOCKS = LEADS // BLOCK


def remote(src, dst, send, recv, device):
    return pltpu.make_async_remote_copy(
        src_ref=src, dst_ref=dst, send_sem=send, recv_sem=recv, device_id=device, device_id_type=MESH
    )


def kernel(
    cur_hbm, arch_hbm, obs_hbm, w_hbm, blur_hbm, cal_hbm, today_hbm,
    out_ref,
    w_ref, blur_ref, cal_ref, today_ref,
    cur_in, arch, obs, stage, landed, gath, curr, dw, edge_lo, edge_hi, halo_up, halo_dn, season, parts, other, pack, packed,
    pieces, ends,
    local_sem, arch_sem, pair_sem, z_send, z_recv, y_send, y_recv, c_send, c_recv, h_send, h_recv, p_send, p_recv,
    r_send, r_recv, e_send, e_recv,
):
    date, tile = lax.axis_index("date"), lax.axis_index("tile")
    row, depth, core = date // 8, (date // 2) % 4, date % 2
    chip = row * 4 + depth
    tiles = 8

    def at(dy, dz):
        return ((((row + dy) % 4) * 4 + (depth + dz) % 4) * 2 + core, tile)

    def chip_at(dy, dz):
        return ((row + dy) % 4) * 4 + (depth + dz) % 4

    partner = (date + 1 - 2 * core, tile)
    others = [(dy, dz) for dy in range(4) for dz in range(4) if (dy, dz) != (0, 0)]

    load_cur = pltpu.make_async_copy(cur_hbm, cur_in, local_sem.at[0])
    load_cur.start()
    small = []
    for i, (src, dst) in enumerate(((w_hbm, w_ref), (blur_hbm, blur_ref), (cal_hbm, cal_ref), (today_hbm, today_ref))):
        copy = pltpu.make_async_copy(src, dst, local_sem.at[2 + i])
        copy.start()
        small.append(copy)
    barrier = pltpu.get_barrier_semaphore()
    for step in (1, 3, 2):
        pl.semaphore_signal(barrier, inc=1, device_id=at(0, step), device_id_type=MESH)
        pl.semaphore_signal(barrier, inc=1, device_id=at(step, 0), device_id_type=MESH)
    pl.semaphore_signal(barrier, inc=1, device_id=partner, device_id_type=MESH)

    @pl.when(tile > 0)
    def _():
        pl.semaphore_signal(barrier, inc=1, device_id=(date, tile - 1), device_id_type=MESH)

    @pl.when(tile < tiles - 1)
    def _():
        pl.semaphore_signal(barrier, inc=1, device_id=(date, tile + 1), device_id_type=MESH)

    loads = []
    for j, (t0, n, _, _) in enumerate(CHUNKS):
        copy = pltpu.make_async_copy(arch_hbm.at[:, pl.ds(t0, n)], arch.at[:, pl.ds(t0, n)], arch_sem.at[j])
        copy.start()
        loads.append(copy)
    load_obs = pltpu.make_async_copy(obs_hbm, obs, local_sem.at[1])
    load_obs.start()

    load_cur.wait()
    for x in range(4):
        for mine in range(2):
            cycle = core if mine else 1 - core
            values = cur_in[cycle, :, :, x, :].reshape(128, LEADS).T
            if mine:
                gath[:, row, depth, core * 4 + x, :] = values
            else:
                stage[:, x, :] = values

    pl.semaphore_wait(barrier, 7 + jnp.where(tile > 0, 1, 0) + jnp.where(tile < tiles - 1, 1, 0))

    pair = remote(stage, landed, pair_sem.at[0], pair_sem.at[1], partner)
    pair.start()

    zero = jnp.zeros((8, 128), jnp.float32)
    for k in range(REACH):
        for side in (k, LEADS + REACH + k):
            for i in range(8):
                dw[side, i] = zero
            halo_up[side] = zero
            halo_dn[side] = zero

    @pl.when(tile == 0)
    def _():
        for t in range(LEADS):
            halo_up[REACH + t] = zero

    @pl.when(tile == tiles - 1)
    def _():
        for t in range(LEADS):
            halo_dn[REACH + t] = zero

    for copy in small:
        copy.wait()
    sub = lax.broadcasted_iota(jnp.int32, (8, 128), 0)
    lane = lax.broadcasted_iota(jnp.int32, (8, 128), 1)
    days = jnp.zeros((8, 128), jnp.float32)
    for i in range(8):
        gap = (cal_ref[i % 4] - today_ref[i // 4]).astype(jnp.float32)
        days = jnp.where(sub == i, gap, days)
    season[...] = 0.5 * (1.0 - jnp.cos(2.0 * math.pi * days / 365.0))

    pair.wait_recv()
    for x in range(4):
        gath[:, row, depth, (1 - core) * 4 + x, :] = landed[:, x, :]

    def part(j, y, z):
        t0, n = CHUNKS[j][:2]
        return gath.at[pl.ds(t0, n), y, z]

    def first(j, d):
        mine = part(j, row, depth)
        to = at(d, 0) if CHUNKS[j][2] else at(0, d)
        return remote(mine, mine, z_send.at[j, d - 1], z_recv.at[j, d - 1], to)

    def first_wait(j, d):
        here = part(j, (row + 4 - d) % 4, depth) if CHUNKS[j][2] else part(j, row, (depth + 4 - d) % 4)
        remote(here, here, z_send.at[j, d - 1], z_recv.at[j, d - 1], partner).wait_recv()

    every = slice(None)
    halves = (pl.ds(0, 2), pl.ds(2, 2))

    def line(j, d, which):
        if CHUNKS[j][2]:
            return part(j, which, (depth + 4 - d) % 4)
        return part(j, (row + 4 - d) % 4, which)

    def ahead(j, d):
        return at(0, d) if CHUNKS[j][2] else at(d, 0)

    def second(j, d):
        mine = line(j, 0, every)
        return remote(mine, mine, y_send.at[j, d - 1], y_recv.at[j, d - 1], ahead(j, d))

    def second_wait(j, d):
        here = line(j, d, every)
        remote(here, here, y_send.at[j, d - 1], y_recv.at[j, d - 1], partner).wait_recv()

    def forward(j, up):
        half, sem = (line(j, 1, halves[0]), 1) if up else (line(j, 3, halves[1]), 3)
        return remote(half, half, y_send.at[j, sem], y_recv.at[j, sem], ahead(j, 1 if up else 3))

    def forward_wait(j, up):
        half, sem = (line(j, 2, halves[0]), 1) if up else (line(j, 2, halves[1]), 3)
        remote(half, half, y_send.at[j, sem], y_recv.at[j, sem], partner).wait_recv()

    def c_copy(j, cycle):
        t0, n = CHUNKS[j][:2]
        block = curr.at[cycle, pl.ds(t0, n)]
        return remote(block, block, c_send.at[j], c_recv.at[j], partner)

    def h_copy(j, up):
        t0, n = CHUNKS[j][:2]
        if up:
            return remote(
                edge_hi.at[pl.ds(t0, n)], halo_up.at[pl.ds(REACH + t0, n)], h_send.at[j, 0], h_recv.at[j, 0], (date, tile + 1)
            )
        return remote(
            edge_lo.at[pl.ds(t0, n)], halo_dn.at[pl.ds(REACH + t0, n)], h_send.at[j, 1], h_recv.at[j, 1], (date, tile - 1)
        )

    def p_copy(b):
        return remote(
            parts.at[1 - core, pl.ds(b * BLOCK, BLOCK)], other.at[pl.ds(b * BLOCK, BLOCK)], p_send.at[b], p_recv.at[b], partner
        )

    def r_copy(b, o):
        dy, dz = others[o]
        return remote(packed.at[b, chip_at(dy, dz)], pieces.at[b, o], r_send.at[b], r_recv.at[b], at(dy, dz))

    plain = [j for j in range(len(CHUNKS)) if not CHUNKS[j][2]]
    turned = [j for j in range(len(CHUNKS)) if CHUNKS[j][2]]
    for j in turned + plain:
        for d in (2, 1, 3):
            first(j, d).start()
    def relay(j):
        second_wait(j, 1)
        forward(j, True).start()
        second_wait(j, 3)
        forward(j, False).start()

    def onward(j):
        for d in (1, 3, 2):
            first_wait(j, d)
        for d in (1, 3) if CHUNKS[j][3] else (2, 1, 3):
            second(j, d).start()

    def transpose(j):
        t0, n = CHUNKS[j][:2]
        if not CHUNKS[j][3]:
            for d in (1, 3, 2):
                second_wait(j, d)
        else:
            forward_wait(j, True)
            forward_wait(j, False)

        def turn(t, carry):
            curr[core, t] = gath[t].reshape(128, 128).T.reshape(16, 8, 128)
            return carry

        lax.fori_loop(t0, t0 + n, turn, 0, unroll=True)
        c_copy(j, core).start()

    def differences(j):
        t0, n = CHUNKS[j][:2]
        loads[j].wait()
        c_copy(j, 1 - core).wait_recv()

        def one(t, carry):
            sums = {}
            for p in range(16):
                now = curr[0, t, p], curr[1, t, p]
                for d in range(4):
                    past = arch[d, t, p]
                    for c in range(2):
                        gap = now[c] - past
                        term = gap * gap * w_ref[p]
                        sums[c, d] = term if p == 0 else sums[c, d] + term
            for d in range(4):
                for c in range(2):
                    v = sums[c, d]
                    v = (
                        v
                        + jnp.where(lane > 0, pltpu.roll(v, 1, 1), 0.0)
                        + jnp.where(lane < 127, pltpu.roll(v, 127, 1), 0.0)
                    )
                    i = c * 4 + d
                    dw[t + REACH, i] = v
                    edge_lo[t, pl.ds(i, 1)] = v[0:1]
                    edge_hi[t, pl.ds(i, 1)] = v[7:8]
            return carry

        lax.fori_loop(t0, t0 + n, one, 0)

        @pl.when(tile < tiles - 1)
        def _():
            h_copy(j, True).start()

        @pl.when(tile > 0)
        def _():
            h_copy(j, False).start()

    scored, sent, seen = set(), [0], set()

    def scores(j):
        t0, n = CHUNKS[j][:2]
        if not seen:
            load_obs.wait()

        @pl.when(tile > 0)
        def _():
            h_copy(j, True).wait_recv()

        @pl.when(tile < tiles - 1)
        def _():
            h_copy(j, False).wait_recv()

        def one(t, carry):
            above, below = halo_up[t], halo_dn[t]
            for k in range(1, 2 * REACH + 1):
                above = above + halo_up[t + k]
                below = below + halo_dn[t + k]
            spread = blur_ref[t]
            inverse = 1.0 / jnp.full((8, 128), spread, jnp.float32)
            for c in range(2):
                dist = []
                for d in range(4):
                    i = c * 4 + d
                    v = dw[t, i]
                    for k in range(1, 2 * REACH + 1):
                        v = v + dw[t + k, i]
                    up = jnp.where(sub == 0, jnp.broadcast_to(above[i : i + 1], (8, 128)), pltpu.roll(v, 1, 0))
                    down = jnp.where(sub == 7, jnp.broadcast_to(below[i : i + 1], (8, 128)), pltpu.roll(v, 7, 0))
                    v = (v + up + down) * (1.0 / (16.0 * 9.0 * (2 * REACH + 1)))
                    dist.append(v + jnp.broadcast_to(season[pl.ds(i, 1)], (8, 128)))
                low = jnp.minimum(jnp.minimum(dist[0], dist[1]), jnp.minimum(dist[2], dist[3]))
                den = num = None
                for d in range(4):
                    e = jnp.exp((low - dist[d]) * inverse)
                    f = e * obs[d, t]
                    den = e if d == 0 else den + e
                    num = f if d == 0 else num + f
                parts[c, t, 0] = low - spread * jnp.log(den)
                parts[c, t, 1] = num / den
            return carry

        seen.update(range(t0, t0 + n))
        ready = [
            t for t in range(LEADS)
            if t not in scored and all(u in seen for u in range(max(t - REACH, 0), min(t + REACH + 1, LEADS)))
        ]
        while ready:
            stop = ready[0] + 1
            while stop in ready:
                stop += 1
            lax.fori_loop(ready[0], stop, one, 0, unroll=2)
            scored.update(range(ready[0], stop))
            ready = [t for t in ready if t >= stop]
        while sent[0] < BLOCKS and all(t in scored for t in range(sent[0] * BLOCK, (sent[0] + 1) * BLOCK)):
            p_copy(sent[0]).start()
            sent[0] += 1

    def combine(b):
        p_copy(b).wait_recv()

        def one(s, carry):
            t = b * BLOCK + s
            spread = blur_ref[t]
            a0, r0 = parts[core, t, 0], parts[core, t, 1]
            a1, r1 = other[t, 0], other[t, 1]
            low = jnp.minimum(a0, a1)
            e0, e1 = jnp.exp((low - a0) / spread), jnp.exp((low - a1) / spread)
            den = e0 + e1
            pack[0, :, s, :] = low - spread * jnp.log(den)
            pack[1, :, s, :] = (e0 * r0 + e1 * r1) / den
            return carry

        lax.fori_loop(0, BLOCK, one, 0, unroll=True)
        packed[b] = pack[...].reshape(128, 128).T.reshape(16, 8, 128)
        for o in range(15):
            r_copy(b, o).start()

    acts = {"F": onward, "R": relay, "T": transpose, "D": differences, "S": scores}
    combined = 0
    for kind, j in STEPS:
        due = sent[0]
        acts[kind](j)
        if kind != "R":
            while combined < due:
                combine(combined)
                combined += 1
    while combined < BLOCKS:
        combine(combined)
        combined += 1

    def e_copy(b, cycle):
        return remote(ends.at[cycle, b], ends.at[cycle, b], e_send.at[b], e_recv.at[b], partner)

    for b in range(BLOCKS):
        here = pieces.at[b]
        remote(here, here, r_send.at[b], r_recv.at[b], partner).wait_recv()
        spread = jnp.zeros((8, 128), jnp.float32)
        for s in range(BLOCK):
            spread = jnp.where(lane % BLOCK == s, blur_ref[b * BLOCK + s], spread)
        terms = [packed[b, chip]] + [pieces[b, o] for o in range(15)]
        low = functools.reduce(jnp.minimum, terms)
        den = num = None
        for i, v in enumerate(terms):
            e = jnp.exp((low - v) / spread)
            f = pltpu.roll(e, 64, 1) * v
            den = e if i == 0 else den + e
            num = f if i == 0 else num + f
        ends[core, b] = num / pltpu.roll(den, 64, 1)
        e_copy(b, core).start()

    for b in range(BLOCKS):
        e_copy(b, 1 - core).wait_recv()
    for c in range(2):
        blocks = []
        for b in range(BLOCKS):
            v = ends[c, b]
            blocks.append(jnp.where(core == 0, v, pltpu.roll(v, 4, 0)))
        for y in range(8):
            v = jnp.zeros((8, 128), jnp.float32)
            for b in range(BLOCKS):
                shift = (b * BLOCK - 64 - y * BLOCK) % 128
                moved = blocks[b] if shift == 0 else pltpu.roll(blocks[b], shift, 1)
                v = jnp.where(lane // BLOCK == b, moved, v)
            out_ref[c, y] = v[0:4, 0:LEADS]

    pair.wait_send()
    for j in range(len(CHUNKS)):
        for d in (1, 2, 3):
            first(j, d).wait_send()
            if d != 2 or not CHUNKS[j][3]:
                second(j, d).wait_send()
        if CHUNKS[j][3]:
            forward(j, True).wait_send()
            forward(j, False).wait_send()
        c_copy(j, core).wait_send()

    @pl.when(tile < tiles - 1)
    def _():
        for j in range(len(CHUNKS)):
            h_copy(j, True).wait_send()

    @pl.when(tile > 0)
    def _():
        for j in range(len(CHUNKS)):
            h_copy(j, False).wait_send()

    for b in range(BLOCKS):
        p_copy(b).wait_send()
        e_copy(b, core).wait_send()
        here = pieces.at[b]
        remote(here, here, r_send.at[b], r_recv.at[b], partner).wait_send()


def local(current, archive, reports, weights, blur, calendar, today):
    count = len(CHUNKS)
    f32 = jnp.float32
    dma = pltpu.SemaphoreType.DMA
    leads = LEADS + 2 * REACH
    out = pl.pallas_call(
        kernel,
        out_shape=jax.ShapeDtypeStruct((2, 8, 4, LEADS), f32),
        in_specs=[pl.BlockSpec(memory_space=pl.ANY)] * 7,
        out_specs=pl.BlockSpec(memory_space=pltpu.VMEM),
        scratch_shapes=[
            pltpu.SMEM((16,), f32), pltpu.SMEM((LEADS,), f32), pltpu.SMEM((4,), jnp.int32), pltpu.SMEM((2,), jnp.int32),
            pltpu.VMEM((2, 16, 8, 4, LEADS), f32),
            pltpu.VMEM((4, LEADS, 16, 8, 128), f32),
            pltpu.VMEM((4, LEADS, 8, 128), f32),
            pltpu.VMEM((LEADS, 4, 128), f32),
            pltpu.VMEM((LEADS, 4, 128), f32),
            pltpu.VMEM((LEADS, 4, 4, 8, 128), f32),
            pltpu.VMEM((2, LEADS, 16, 8, 128), f32),
            pltpu.VMEM((leads, 8, 8, 128), f32),
            pltpu.VMEM((LEADS, 8, 128), f32),
            pltpu.VMEM((LEADS, 8, 128), f32),
            pltpu.VMEM((leads, 8, 128), f32),
            pltpu.VMEM((leads, 8, 128), f32),
            pltpu.VMEM((8, 128), f32),
            pltpu.VMEM((2, LEADS, 2, 8, 128), f32),
            pltpu.VMEM((LEADS, 2, 8, 128), f32),
            pltpu.VMEM((2, 8, BLOCK, 128), f32),
            pltpu.VMEM((BLOCKS, 16, 8, 128), f32),
            pltpu.VMEM((BLOCKS, 15, 8, 128), f32),
            pltpu.VMEM((2, BLOCKS, 8, 128), f32),
            dma((6,)),
            dma((count,)),
            dma((2,)),
            dma((count, 3)), dma((count, 3)),
            dma((count, 4)), dma((count, 4)),
            dma((count,)), dma((count,)),
            dma((count, 2)), dma((count, 2)),
            dma((BLOCKS,)), dma((BLOCKS,)),
            dma((BLOCKS,)), dma((BLOCKS,)),
            dma((BLOCKS,)), dma((BLOCKS,)),
        ],
        compiler_params=pltpu.CompilerParams(
            collective_id=0, has_side_effects=True, vmem_limit_bytes=60 * 2**20
        ),
    )(jnp.transpose(current, (0, 2, 3, 4, 1)), archive, reports, weights, blur, calendar, today)
    return jnp.transpose(out, (0, 3, 1, 2))


def solution(mesh):
    placed = (
        P(None, None, None, "tile", "date"),
        P("date", None, None, "tile", None),
        P("date", None, "tile", None),
        P(),
        P(),
        P("date"),
        P(),
    )
    return jax.shard_map(
        local, mesh=mesh, in_specs=placed, out_specs=P(None, None, "tile", "date"), check_vma=False
    )
```
